512 devices in a mesh: gx: 64 (over y, x, z_hi), gy: 8 (over z_lo, core).
Axes of the slice: x: 4, y: 8, z: 8 (z_hi: 2, z_lo: 4; z = z_hi * 4 + z_lo), core: 2. Of those that a mesh axis runs over, the one named last changes fastest.
Arguments:
- position: float32 [3, 64, 128, 1024], P(None, None, 'gx', 'gy'), may hold values from 0 to 1
- velocity: float32 [3, 64, 128, 1024], P(None, None, 'gx', 'gy'), may hold values from -4 to 4
- particle_mass: float32 [64, 128, 1024], P(None, 'gx', 'gy'), may hold values from 0.0078125 to 0.03125
- counts: int32 [128, 1024], P('gx', 'gy'), may hold values from 16 to 64
Outputs:
- density: float32 [64, 128, 1024], P(None, 'gx', 'gy')
- acceleration: float32 [3, 64, 128, 1024], P(None, None, 'gx', 'gy')
The draws below stay inside these ranges and needn't reach their ends.
All inputs are finite; a program needn't handle non-finite values.
Results may differ from the reference program's by a relative error of at most 0.0003.
Values sent between devices are 32-bit elements; how exact they have to be, the bound alone decides.
A program may use at most 64 MiB of HBM per device.

```python
import math
import jax
import jax.numpy as jnp
from jax import lax

P_SIZE = 64
NCX = 128
NCY = 1024


def plant(result, stream_key, least, top_value):
    shape = result.shape
    place = [jax.random.randint(jax.random.fold_in(stream_key, axis), (), 0, shape[axis]) for axis in range(len(shape))]
    result = result.at[tuple(place)].set(least)
    longest = shape.index(max(shape))
    place[longest] = (place[longest] + 1) % shape[longest]
    return result.at[tuple(place)].set(top_value)


def level_of(rng, shape, shards, smallest, high):
    level = 1.0
    for axis_at, parts in shards:
        steps = jax.random.uniform(jax.random.fold_in(jax.random.fold_in(rng, 6), axis_at), (parts,), jnp.float32, smallest / len(shards), high / len(shards))
        level = level * jnp.repeat(jnp.exp(steps), shape[axis_at] // parts).reshape((-1,) + (1,) * (len(shape) - 1 - axis_at))
    return level


def bell_draw(rng, shape, width, bound, split=(), kind=jnp.bfloat16):
    entries = jax.random.normal(rng, shape, jnp.float32) * width
    if len(split) > 0:
        entries = level_of(rng, shape, split, -0.22, 0.18) * entries
    return jnp.clip(entries, min=-bound, max=bound).astype(kind)


def setup_inputs(seed: int = 0) -> dict:
    streams_of = jax.random.split(jax.random.key(seed), 5)
    return {
        "position": jnp.clip(1.0 * jax.random.uniform(streams_of[0], (3, P_SIZE, NCX, NCY), jnp.float32) ** level_of(streams_of[0], (3, P_SIZE, NCX, NCY), ((2, 64), (3, 8)), -0.2, 0.2), 0.0, 1.0),
        "velocity": bell_draw(streams_of[1], (3, P_SIZE, NCX, NCY), 1.0, 4.0, ((2, 64), (3, 8)), jnp.float32),
        "particle_mass": jnp.clip(jnp.exp(math.log(0.03125) - 1.3862944 * jax.random.uniform(streams_of[2], (P_SIZE, NCX, NCY), jnp.float32) ** level_of(streams_of[2], (P_SIZE, NCX, NCY), ((1, 64), (2, 8)), -0.2, 0.2)), 0.0078125, 0.03125),
        "counts": plant(jax.random.randint(streams_of[3], (NCX, NCY), P_SIZE // 4, P_SIZE + 1), jax.random.fold_in(streams_of[3], 1), P_SIZE // 4, P_SIZE).astype(jnp.int32),
    }


KERNEL_NORM = 21.0 / (2.0 * 3.141592653589793)
REST_DENSITY = 0.5
VISCOSITY = 0.5
SMOOTHING = 0.5
WALL_STIFFNESS = 4.0

def pair_geometry(own_cells, near_cells, shift_x, shift_y):
    sep_x = own_cells[0][:, None] - near_cells[0][None, :] - shift_x
    sep_y = own_cells[1][:, None] - near_cells[1][None, :] - shift_y
    sep_z = own_cells[2][:, None] - near_cells[2][None, :]
    distance_sq = sep_x * sep_x + sep_y * sep_y + sep_z * sep_z
    distance = jnp.sqrt(distance_sq)
    spline = jnp.maximum(1.0 - distance, 0.0)
    return (sep_x, sep_y, sep_z, distance_sq, distance, spline)

def density_terms(own_cells, near_cells, shift_x, shift_y):
    geometry = pair_geometry(own_cells, near_cells, shift_x, shift_y)
    spline_sq = geometry[5] * geometry[5]
    kernel = KERNEL_NORM * spline_sq * spline_sq * (1.0 + 4.0 * geometry[4])
    return lax.optimization_barrier(jnp.sum(near_cells[6][None, :] * kernel, axis=1))

def pressure_term(density_value):
    return (density_value - REST_DENSITY) / (density_value * density_value)

def force_terms(own_cells, own_rho, near_cells, near_rho, shift_x, shift_y):
    sep_x, sep_y, sep_z, distance_sq, distance, spline = pair_geometry(own_cells, near_cells, shift_x, shift_y)
    closing = (own_cells[3][:, None] - near_cells[3][None, :]) * sep_x + (own_cells[4][:, None] - near_cells[4][None, :]) * sep_y + (own_cells[5][:, None] - near_cells[5][None, :]) * sep_z
    approach = SMOOTHING * jnp.minimum(closing, 0.0) / (distance_sq + 0.01 * SMOOTHING * SMOOTHING)
    mean_rho = 0.5 * (own_rho[:, None] + near_rho[None, :])
    damping = -VISCOSITY * approach / mean_rho
    kernel_slope = -20.0 * KERNEL_NORM * spline * spline * spline
    pair_weight = near_cells[6][None, :] * (pressure_term(own_rho)[:, None] + pressure_term(near_rho)[None, :] + damping) * kernel_slope
    return jnp.stack([-lax.optimization_barrier(jnp.sum(pair_weight * sep_x, axis=1)), -lax.optimization_barrier(jnp.sum(pair_weight * sep_y, axis=1)), -lax.optimization_barrier(jnp.sum(pair_weight * sep_z, axis=1))])

def stencil_density(own_cells, extended):
    width_x = own_cells.shape[2]
    width_y = own_cells.shape[3]
    summed = jnp.zeros(own_cells.shape[1:], jnp.float32)
    for shift_x in (-1, 0, 1):
        for shift_y in (-1, 0, 1):
            near_cells = extended[:, :, 1 + shift_x:1 + shift_x + width_x, 1 + shift_y:1 + shift_y + width_y]
            summed = summed + density_terms(own_cells, near_cells, float(shift_x), float(shift_y))
    return summed

def stencil_force(own_cells, own_rho, extended, halo_rho):
    width_x = own_cells.shape[2]
    width_y = own_cells.shape[3]
    summed = jnp.zeros((3,) + own_cells.shape[1:], jnp.float32)
    for shift_x in (-1, 0, 1):
        for shift_y in (-1, 0, 1):
            near_cells = extended[:, :, 1 + shift_x:1 + shift_x + width_x, 1 + shift_y:1 + shift_y + width_y]
            near_rho = halo_rho[:, 1 + shift_x:1 + shift_x + width_x, 1 + shift_y:1 + shift_y + width_y]
            summed = summed + force_terms(own_cells, own_rho, near_cells, near_rho, float(shift_x), float(shift_y))
    return summed

def reference(position, velocity, particle_mass, counts):
    slot_count = position.shape[1]
    occupied = jnp.arange(slot_count, dtype=jnp.int32)[:, None, None] < counts[None]
    live_mass = jnp.where(occupied, particle_mass, 0.0)
    fields = jnp.concatenate([position, velocity, live_mass[None]], axis=0)
    padded = jnp.pad(fields, ((0, 0), (0, 0), (0, 0), (1, 1)))

    def column_fields(column):
        columns = [lax.dynamic_index_in_dim(padded, (column + shift) % NCX, axis=2, keepdims=True) for shift in (-1, 0, 1)]
        return jnp.concatenate(columns, axis=2)

    def column_density(column):
        extended = column_fields(column)
        return stencil_density(extended[:, :, 1:2, 1:-1], extended)[:, 0]
    column_ids = jnp.arange(NCX, dtype=jnp.int32)
    rho_raw = jnp.transpose(lax.map(column_density, column_ids), (1, 0, 2))
    rho_safe = jnp.where(occupied, rho_raw, 1.0)
    padded_rho = jnp.pad(rho_safe, ((0, 0), (0, 0), (1, 1)), constant_values=1.0)

    def column_force(column):
        extended = column_fields(column)
        columns = [lax.dynamic_index_in_dim(padded_rho, (column + shift) % NCX, axis=1, keepdims=True) for shift in (-1, 0, 1)]
        halo_rho = jnp.concatenate(columns, axis=1)
        return stencil_force(extended[:, :, 1:2, 1:-1], halo_rho[:, 1:2, 1:-1], extended, halo_rho)[:, :, 0]
    acceleration = jnp.transpose(lax.map(column_force, column_ids), (1, 2, 0, 3))
    height = jnp.arange(NCY, dtype=jnp.int32).astype(jnp.float32)[None, None, :] + position[1]
    near_floor = jnp.maximum(1.0 - 2.0 * height, 0.0)
    near_ceiling = jnp.maximum(1.0 - 2.0 * (NCY - height), 0.0)
    wall_push = WALL_STIFFNESS * (near_floor * near_floor - near_ceiling * near_ceiling)
    acceleration = jnp.stack([acceleration[0], acceleration[1] + wall_push, acceleration[2]])
    density = jnp.where(occupied, rho_raw, 0.0)
    acceleration = jnp.where(occupied[None], acceleration, 0.0)
    return (density, acceleration)
```

```python
import functools

import jax
import jax.numpy as jnp
from jax import lax
from jax.experimental import pallas as pl
from jax.experimental.pallas import tpu as pltpu
from jax.sharding import PartitionSpec as P

MESH = pl.DeviceIdType.MESH
F32 = jnp.float32
KERNEL_NORM = 21.0 / (2.0 * 3.141592653589793)
REST_DENSITY = 0.5
VISCOSITY = 0.5
SMOOTHING = 0.5
WALL_STIFFNESS = 4.0
TINY = 1e-30
SLOTS = 64
LANES = 128

INNER = ((1, 1, 1, 0), (2, 2, 1, 1), (1, 2, 1, 1), (1, 2, 0, 2), (1, 2, -1, 3))
OTHERS = ((0, 1), (1, 1), (1, 0), (1, -1))
UNITS = len(INNER) + 2 + 6


def pressure_term(rho):
    return (rho - REST_DENSITY) / (rho * rho)


def spline_of(dx, dy, dz):
    dist_sq = jnp.maximum(dx * dx + dy * dy + dz * dz, TINY)
    dist = dist_sq * lax.rsqrt(dist_sq)
    return dist, jnp.maximum(1.0 - dist, 0.0)


def density_pair(dist, spline):
    spline_sq = spline * spline
    return spline_sq * spline_sq * (dist + 0.25)


def lane_ids(rows):
    return lax.broadcasted_iota(jnp.int32, (rows, LANES), 1)


def shifted(cells, shift):
    return cells if shift == 0 else pltpu.roll(cells, (-shift) % LANES, 1)


def wrapped_lane(shift):
    return LANES - 1 if shift > 0 else 0


def kernel(
    gx_count, gy_count,
    pos_ref, vel_ref, mass_ref, counts_ref, rho_out, acc_out,
    near_p, near_v, near_r, got_p, got_v, got_r, edge_own, edge_got, edge_rho, edge_rho_got,
    kept, rho_sum, rho_other, force_sum, force_one, force_other, send_sem, recv_sem,
):
    gx = lax.axis_index("gx")
    gy = lax.axis_index("gy")

    def place(step_x, step_y):
        return (lax.rem(gx + step_x + gx_count, gx_count), lax.rem(gy + step_y + gy_count, gy_count))

    barrier = pltpu.get_barrier_semaphore()
    for step_x in (-1, 0, 1):
        for step_y in (-1, 0, 1):
            if step_x != 0 or step_y != 0:
                pl.semaphore_signal(barrier, inc=1, device_id=place(step_x, step_y), device_id_type=MESH)

    for col in range(2):
        rows = pl.ds(col, SLOTS, stride=2)
        slot = lax.broadcasted_iota(jnp.int32, (SLOTS, LANES), 0)
        occupied = slot < counts_ref[col : col + 1, :]
        near_p[1 + col, 1, 0] = pos_ref[0, rows, :] + float(col)
        near_p[1 + col, 1, 1] = pos_ref[1, rows, :]
        near_p[1 + col, 1, 2] = pos_ref[2, rows, :]
        near_p[1 + col, 1, 3] = jnp.where(occupied, mass_ref[rows, :], 0.0)

    pl.semaphore_wait(barrier, 8)

    copies = []

    def send(index, source, target, step_x, step_y):
        copy = pltpu.make_async_remote_copy(
            src_ref=source, dst_ref=target, send_sem=send_sem.at[index], recv_sem=recv_sem.at[index],
            device_id=place(step_x, step_y), device_id_type=MESH,
        )
        copy.start()
        copies.append(copy)
        return copy

    pos_copies = [
        send(0, near_p.at[1, 1], got_p.at[1], -1, 0),
        send(1, near_p.at[2, 1], got_p.at[0], 1, 0),
    ]

    for col in range(2):
        rows = pl.ds(col, SLOTS, stride=2)
        for axis in range(3):
            near_v[1 + col, 1, axis] = SMOOTHING * vel_ref[axis, rows, :]

    def edge_pack(fields, lane):
        ids = lane_ids(SLOTS)
        halves = []
        for col in range(2):
            pack = jnp.zeros((SLOTS, LANES), F32)
            for index, field in enumerate(fields[col]):
                pack = jnp.where(ids == index, field[:, lane : lane + 1], pack)
            halves.append(pack)
        return jnp.concatenate(halves, axis=0).T[0:8, :]

    own_fields = [
        [near_p[1 + col, 1, f] for f in range(4)] + [near_v[1 + col, 1, f] for f in range(3)] for col in range(2)
    ]
    for edge, lane in ((0, 0), (1, LANES - 1)):
        edge_own[edge] = edge_pack(own_fields, lane)
    edge_copies = []
    for edge, step_y in ((0, -1), (1, 1)):
        for which, step_x in enumerate((0, 1, -1)):
            edge_copies.append(
                send(2 + edge * 3 + which, edge_own.at[edge], edge_got.at[1 - edge, which], step_x, step_y)
            )
    vel_copies = [
        send(8, near_v.at[1, 1], got_v.at[1], -1, 0),
        send(9, near_v.at[2, 1], got_v.at[0], 1, 0),
    ]

    def shift_positions(column, columns, first):
        for shift in (-1, 0, 1):
            if first and shift == 0:
                continue
            ids = lane_ids(SLOTS)
            near_p[column, 1 + shift, 0] = shifted(columns[0], shift)
            near_p[column, 1 + shift, 1] = shifted(columns[1], shift) + float(shift)
            near_p[column, 1 + shift, 2] = shifted(columns[2], shift)
            mass = shifted(columns[3], shift)
            if shift != 0:
                mass = jnp.where(ids == wrapped_lane(shift), 0.0, mass)
            near_p[column, 1 + shift, 3] = mass

    for column in (1, 2):
        shift_positions(column, [near_p[column, 1, f] for f in range(4)], True)

    def density_unit(unit, own, near, near_shift, other, fresh):
        for half in range(2):
            rows = slice(32 * half, 32 * half + 32)
            own_x, own_y, own_z, own_m = (near_p[own, 1, f, rows, :] for f in range(4))

            def step(j, total):
                near_x, near_y, near_z, near_m = (near_p[near, near_shift, f, pl.ds(j, 1), :] for f in range(4))
                dist, spline = spline_of(own_x - near_x, own_y - near_y, own_z - near_z)
                kept[unit, j, rows, :] = spline
                pair = density_pair(dist, spline)
                if other is not None:
                    back = (pair * own_m).reshape(4, 8, LANES).sum(axis=0)
                    if half == 0 and fresh:
                        rho_other[other, j] = back
                    else:
                        rho_other[other, j] += back
                return total + pair * near_m

            total = lax.fori_loop(0, SLOTS, step, jnp.zeros((32, LANES), F32), unroll=2)
            rho_sum[own - 1, rows, :] += total

    rho_sum[...] = jnp.zeros_like(rho_sum)
    seen = set()
    for unit, (own, near, shift, other) in enumerate(INNER):
        density_unit(unit, own, near, 1 + shift, other, other not in seen)
        seen.add(other)

    def self_density(col, carry):
        density_unit(len(INNER) + col, 1 + col, 1 + col, 1, None, True)
        return carry

    lax.fori_loop(0, 2, self_density, 0)

    for copy in pos_copies:
        copy.wait()
    for side, move in ((0, -2.0), (1, 2.0)):
        shift_positions(3 * side, [got_p[side, 0] + move] + [got_p[side, f] for f in range(1, 4)], False)

    def outer_density(index, carry):
        side = index // 3
        density_unit(len(INNER) + 2 + index, 1 + side, 3 * side, index % 3, None, True)
        return carry

    lax.fori_loop(0, 6, outer_density, 0)

    for copy in edge_copies:
        copy.wait()
    left_half = lane_ids(1) < SLOTS

    def edge_rows(edge):
        inside = jnp.where(gy == 0, 0.0, 1.0) if edge == 0 else jnp.where(gy == gy_count - 1, 0.0, 1.0)
        shift = -1.0 if edge == 0 else 1.0
        blocks = []
        for block in range(2):
            rows = []
            for f in range(7):
                if block == 0:
                    row = edge_got[edge, 0, f : f + 1, :]
                else:
                    right = edge_got[edge, 2, f : f + 1, :]
                    left = edge_got[edge, 1, f : f + 1, :]
                    if f == 0:
                        right = right + 2.0
                        left = left - 2.0
                    row = jnp.where(left_half, right, left)
                if f == 1:
                    row = row + shift
                if f == 3:
                    row = row * inside
                rows.append(row)
            blocks.append(rows)
        return blocks

    def edge_lane(edge):
        return 0 if edge == 0 else LANES - 1

    for edge in range(2):
        lane = edge_lane(edge)
        blocks = edge_rows(edge)
        for col in range(2):
            own_x, own_y, own_z = (near_p[1 + col, 1, f][:, lane : lane + 1] for f in range(3))
            total = jnp.zeros((SLOTS, LANES), F32)
            for rows in blocks:
                dist, spline = spline_of(own_x - rows[0], own_y - rows[1], own_z - rows[2])
                total = total + density_pair(dist, spline) * rows[3]
            summed = jnp.sum(total, axis=1, keepdims=True)
            rho_sum[col] += jnp.where(lane_ids(SLOTS) == lane, summed, 0.0)

    for slot, (col, shift) in enumerate(OTHERS):
        back = jnp.sum(rho_other[slot], axis=1)
        if shift != 0:
            back = jnp.where(lane_ids(SLOTS) == wrapped_lane(shift), 0.0, back)
        rho_sum[col] += shifted(back, -shift)

    for col in range(2):
        occupied = near_p[1 + col, 1, 3] > 0.0
        rho = (4.0 * KERNEL_NORM) * rho_sum[col]
        rho_out[pl.ds(col, SLOTS, stride=2), :] = jnp.where(occupied, rho, 0.0)
        rho = jnp.where(occupied, rho, 1.0)
        near_r[1 + col, 1, 0] = rho

    rho_copies = [
        send(10, near_r.at[1, 1, 0], got_r.at[1], -1, 0),
        send(11, near_r.at[2, 1, 0], got_r.at[0], 1, 0),
    ]
    own_rho = [[near_r[1 + col, 1, 0]] for col in range(2)]
    for edge, lane in ((0, 0), (1, LANES - 1)):
        edge_rho[edge] = edge_pack(own_rho, lane)
    edge_rho_copies = []
    for edge, step_y in ((0, -1), (1, 1)):
        for which, step_x in enumerate((0, 1, -1)):
            edge_rho_copies.append(
                send(12 + edge * 3 + which, edge_rho.at[edge], edge_rho_got.at[1 - edge, which], step_x, step_y)
            )

    def shift_rest(column, velocity, rho, first):
        for shift in (-1, 0, 1):
            if not (first and shift == 0):
                for f in range(3):
                    near_v[column, 1 + shift, f] = shifted(velocity[f], shift)
                near_r[column, 1 + shift, 0] = shifted(rho, shift)
            near_r[column, 1 + shift, 1] = pressure_term(shifted(rho, shift))

    for column in (1, 2):
        shift_rest(column, [near_v[column, 1, f] for f in range(3)], near_r[column, 1, 0], True)

    def strength_of(own, near, sep, dist_sq):
        closing = (near[4] - own[4]) * sep[0] + (near[5] - own[5]) * sep[1] + (near[6] - own[6]) * sep[2]
        damping = jnp.maximum(closing, 0.0) / ((dist_sq + 0.01 * SMOOTHING * SMOOTHING) * (own[7] + near[7]))
        return own[8] + near[8] + (2.0 * VISCOSITY) * damping

    def force_unit(unit, own_col, near_col, near_shift, other, fresh):
        def quarter(part, fresh_part):
            rows = pl.ds(pl.multiple_of(16 * part, 16), 16)
            own = (
                [near_p[own_col, 1, f, rows, :] for f in range(4)]
                + [near_v[own_col, 1, f, rows, :] for f in range(3)]
                + [near_r[own_col, 1, f, rows, :] for f in range(2)]
            )

            def step(j, totals):
                row = pl.ds(j, 1)
                near = (
                    [near_p[near_col, near_shift, f, row, :] for f in range(4)]
                    + [near_v[near_col, near_shift, f, row, :] for f in range(3)]
                    + [near_r[near_col, near_shift, f, row, :] for f in range(2)]
                )
                spline = kept[unit, j, rows, :]
                sep = [own[f] - near[f] for f in range(3)]
                dist = 1.0 - spline
                weight = strength_of(own, near, sep, dist * dist) * (spline * spline * spline) * near[3]
                if other is not None:
                    weight = weight * own[3]
                terms = [weight * sep[f] for f in range(3)]
                if other is not None:
                    for f in range(3):
                        back = terms[f][0:8] + terms[f][8:16]
                        if fresh_part:
                            force_other[f, other, j] = back
                        else:
                            force_other[f, other, j] += back
                return tuple(totals[f] + terms[f] for f in range(3))

            totals = lax.fori_loop(0, SLOTS, step, tuple(jnp.zeros((16, LANES), F32) for _ in range(3)), unroll=2)
            target = force_one if other is None else force_sum
            for f in range(3):
                target[own_col - 1, f, rows, :] += totals[f]

        if other is not None and fresh:
            quarter(0, True)
            lax.fori_loop(1, 4, lambda part, carry: (quarter(part, False), carry)[1], 0)
        else:
            lax.fori_loop(0, 4, lambda part, carry: (quarter(part, False), carry)[1], 0)

    force_sum[...] = jnp.zeros_like(force_sum)
    force_one[...] = jnp.zeros_like(force_one)
    seen = set()
    for unit, (own, near, shift, other) in enumerate(INNER):
        force_unit(unit, own, near, 1 + shift, other, other not in seen)
        seen.add(other)

    def self_force(col, carry):
        force_unit(len(INNER) + col, 1 + col, 1 + col, 1, None, True)
        return carry

    lax.fori_loop(0, 2, self_force, 0)

    for copy in vel_copies + rho_copies:
        copy.wait()
    for side in range(2):
        shift_rest(3 * side, [got_v[side, f] for f in range(3)], got_r[side], False)

    def outer_force(index, carry):
        side = index // 3
        force_unit(len(INNER) + 2 + index, 1 + side, 3 * side, index % 3, None, True)
        return carry

    lax.fori_loop(0, 6, outer_force, 0)

    for copy in edge_rho_copies:
        copy.wait()
    for edge in range(2):
        lane = edge_lane(edge)
        blocks = edge_rows(edge)
        for block in range(2):
            if block == 0:
                rho = edge_rho_got[edge, 0, 0:1, :]
            else:
                rho = jnp.where(left_half, edge_rho_got[edge, 2, 0:1, :], edge_rho_got[edge, 1, 0:1, :])
            blocks[block] = blocks[block] + [rho, pressure_term(rho)]
        for col in range(2):
            own = (
                [near_p[1 + col, 1, f][:, lane : lane + 1] for f in range(4)]
                + [near_v[1 + col, 1, f][:, lane : lane + 1] for f in range(3)]
                + [near_r[1 + col, 1, f][:, lane : lane + 1] for f in range(2)]
            )
            totals = [jnp.zeros((SLOTS, LANES), F32) for _ in range(3)]
            for near in blocks:
                sep = [own[f] - near[f] for f in range(3)]
                dist, spline = spline_of(*sep)
                weight = strength_of(own, near, sep, dist * dist) * (spline * spline * spline) * near[3]
                totals = [totals[f] + weight * sep[f] for f in range(3)]
            for f in range(3):
                summed = jnp.sum(totals[f], axis=1, keepdims=True)
                force_one[col, f] += jnp.where(lane_ids(SLOTS) == lane, summed, 0.0)

    for slot, (col, shift) in enumerate(OTHERS):
        for f in range(3):
            force_sum[col, f] -= shifted(jnp.sum(force_other[f, slot], axis=1), -shift)

    for col in range(2):
        rows = pl.ds(col, SLOTS, stride=2)
        mass = near_p[1 + col, 1, 3]
        occupied = mass > 0.0
        per_mass = 1.0 / jnp.where(occupied, mass, 1.0)
        row_id = (gy * LANES + lane_ids(SLOTS)).astype(F32)
        height = row_id + near_p[1 + col, 1, 1]
        near_floor = jnp.maximum(1.0 - 2.0 * height, 0.0)
        near_ceiling = jnp.maximum(1.0 - 2.0 * (float(LANES * gy_count) - height), 0.0)
        push = WALL_STIFFNESS * (near_floor * near_floor - near_ceiling * near_ceiling)
        for f in range(3):
            force = (20.0 * KERNEL_NORM) * (force_sum[col, f] * per_mass + force_one[col, f])
            if f == 1:
                force = force + push
            acc_out[f, rows, :] = jnp.where(occupied, force, 0.0)


def on_device(gx_count, gy_count, position, velocity, particle_mass, counts):
    vmem = pl.BlockSpec(memory_space=pltpu.VMEM)
    column = (SLOTS, LANES)
    rho, acceleration = pl.pallas_call(
        functools.partial(kernel, gx_count, gy_count),
        out_shape=(
            jax.ShapeDtypeStruct((2 * SLOTS, LANES), F32),
            jax.ShapeDtypeStruct((3, 2 * SLOTS, LANES), F32),
        ),
        in_specs=[vmem] * 4,
        out_specs=(vmem, vmem),
        scratch_shapes=[
            pltpu.VMEM((4, 3, 4) + column, F32),
            pltpu.VMEM((4, 3, 3) + column, F32),
            pltpu.VMEM((4, 3, 2) + column, F32),
            pltpu.VMEM((2, 4) + column, F32),
            pltpu.VMEM((2, 3) + column, F32),
            pltpu.VMEM((2,) + column, F32),
            pltpu.VMEM((2, 8, LANES), F32),
            pltpu.VMEM((2, 3, 8, LANES), F32),
            pltpu.VMEM((2, 8, LANES), F32),
            pltpu.VMEM((2, 3, 8, LANES), F32),
            pltpu.VMEM((UNITS, SLOTS) + column, F32),
            pltpu.VMEM((2,) + column, F32),
            pltpu.VMEM((4, SLOTS, 8, LANES), F32),
            pltpu.VMEM((2, 3) + column, F32),
            pltpu.VMEM((2, 3) + column, F32),
            pltpu.VMEM((3, 4, SLOTS, 8, LANES), F32),
            pltpu.SemaphoreType.DMA((18,)),
            pltpu.SemaphoreType.DMA((18,)),
        ],
        compiler_params=pltpu.CompilerParams(
            collective_id=0, has_side_effects=True, vmem_limit_bytes=52 * 1024 * 1024
        ),
        cost_estimate=pl.CostEstimate(flops=400_000_000, bytes_accessed=2_000_000, transcendentals=30_000_000),
    )(
        position.reshape(3, 2 * SLOTS, LANES),
        velocity.reshape(3, 2 * SLOTS, LANES),
        particle_mass.reshape(2 * SLOTS, LANES),
        counts,
    )
    return rho.reshape(SLOTS, 2, LANES), acceleration.reshape(3, SLOTS, 2, LANES)


def solution(mesh):
    in_specs = (
        P(None, None, "gx", "gy"),
        P(None, None, "gx", "gy"),
        P(None, "gx", "gy"),
        P("gx", "gy"),
    )
    out_specs = (P(None, "gx", "gy"), P(None, None, "gx", "gy"))
    step = functools.partial(on_device, mesh.shape["gx"], mesh.shape["gy"])
    return jax.shard_map(step, mesh=mesh, in_specs=in_specs, out_specs=out_specs, check_vma=False)
```

```python
import functools

import jax
import jax.numpy as jnp
from jax import lax
from jax.experimental import pallas as pl
from jax.experimental.pallas import tpu as pltpu
from jax.sharding import PartitionSpec as P

MESH = pl.DeviceIdType.MESH
F32 = jnp.float32
KERNEL_NORM = 21.0 / (2.0 * 3.141592653589793)
REST_DENSITY = 0.5
VISCOSITY = 0.5
SMOOTHING = 0.5
WALL_STIFFNESS = 4.0
TINY = 1e-30
SLOTS = 64
LANES = 128

OTHERS = ((0, 1), (1, -1), (1, 0), (1, 1), (2, -1), (2, 0), (2, 1), (0, 0))
SAME_ROW = (7, 2)
UNITS = 10
DENSITY_ROWS = 32
FORCE_ROWS = 16
DENSITY_UNROLL = 16
FORCE_UNROLL = 16


def pressure_term(rho):
    return (rho - REST_DENSITY) / (rho * rho)


def spline_of(dx, dy, dz):
    dist_sq = jnp.maximum(dx * dx + dy * dy + dz * dz, TINY)
    dist = dist_sq * lax.rsqrt(dist_sq)
    return dist, jnp.maximum(1.0 - dist, 0.0)


def density_pair(dist, spline):
    spline_sq = spline * spline
    return spline_sq * spline_sq * (dist + 0.25)


def strength_of(own, near, sep, dist_sq):
    closing = (near[4] - own[4]) * sep[0] + (near[5] - own[5]) * sep[1] + (near[6] - own[6]) * sep[2]
    damping = jnp.maximum(closing, 0.0) / ((dist_sq + 0.01 * SMOOTHING * SMOOTHING) * (own[7] + near[7]))
    return own[8] + near[8] + (2.0 * VISCOSITY) * damping


def lane_ids(rows):
    return lax.broadcasted_iota(jnp.int32, (rows, LANES), 1)


def shifted(cells, shift):
    return cells if shift == 0 else pltpu.roll(cells, (-shift) % LANES, 1)


def wrapped_lane(shift):
    return LANES - 1 if shift > 0 else 0


def groups_sum(cells):
    total = cells[0:8]
    for first in range(8, cells.shape[0], 8):
        total = total + cells[first : first + 8]
    return total


def kernel(
    gx_count, gy_count,
    pos_ref, vel_ref, mass_ref, counts_ref, rho_out, acc_out,
    near_p, near_v, near_r, got_p, got_v, got_r, back_d, got_d, back_f, got_f,
    edge_own, edge_got, edge_rho, edge_rho_got,
    kept, rho_sum, rho_other, force_sum, force_one, force_other, send_sem, recv_sem,
):
    gx = lax.axis_index("gx")
    gy = lax.axis_index("gy")

    def place(step_x, step_y):
        return (lax.rem(gx + step_x + gx_count, gx_count), lax.rem(gy + step_y + gy_count, gy_count))

    barrier = pltpu.get_barrier_semaphore()
    for step_x in (-1, 0, 1):
        for step_y in (-1, 0, 1):
            if step_x != 0 or step_y != 0:
                pl.semaphore_signal(barrier, inc=1, device_id=place(step_x, step_y), device_id_type=MESH)

    for col in range(2):
        rows = pl.ds(col, SLOTS, stride=2)
        slot = lax.broadcasted_iota(jnp.int32, (SLOTS, LANES), 0)
        occupied = slot < counts_ref[col : col + 1, :]
        near_p[col, 1, 0] = pos_ref[0, rows, :] + float(col)
        near_p[col, 1, 1] = pos_ref[1, rows, :]
        near_p[col, 1, 2] = pos_ref[2, rows, :]
        near_p[col, 1, 3] = jnp.where(occupied, mass_ref[rows, :], 0.0)

    pl.semaphore_wait(barrier, 8)

    def send(index, source, target, step_x, step_y):
        copy = pltpu.make_async_remote_copy(
            src_ref=source, dst_ref=target, send_sem=send_sem.at[index], recv_sem=recv_sem.at[index],
            device_id=place(step_x, step_y), device_id_type=MESH,
        )
        copy.start()
        return copy

    pos_copy = send(0, near_p.at[0, 1], got_p, -1, 0)

    for col in range(2):
        rows = pl.ds(col, SLOTS, stride=2)
        for axis in range(3):
            near_v[col, 1, axis] = SMOOTHING * vel_ref[axis, rows, :]

    def edge_pack(fields, lane):
        ids = lane_ids(SLOTS)
        halves = []
        for col in range(2):
            pack = jnp.zeros((SLOTS, LANES), F32)
            for index, field in enumerate(fields[col]):
                pack = jnp.where(ids == index, field[:, lane : lane + 1], pack)
            halves.append(pack)
        return jnp.concatenate(halves, axis=0).T[0:8, :]

    own_fields = [
        [near_p[col, 1, f] for f in range(4)] + [near_v[col, 1, f] for f in range(3)] for col in range(2)
    ]
    for edge, lane in ((0, 0), (1, LANES - 1)):
        edge_own[edge] = edge_pack(own_fields, lane)
    edge_copies = []
    for edge, step_y in ((0, -1), (1, 1)):
        for which, step_x in enumerate((0, 1, -1)):
            edge_copies.append(
                send(2 + edge * 3 + which, edge_own.at[edge], edge_got.at[1 - edge, which], step_x, step_y)
            )
    vel_copy = send(1, near_v.at[0, 1], got_v, -1, 0)

    rho_sum[...] = jnp.zeros_like(rho_sum)
    rho_other[...] = jnp.zeros_like(rho_other)
    force_sum[...] = jnp.zeros_like(force_sum)
    force_one[...] = jnp.zeros_like(force_one)
    force_other[...] = jnp.zeros_like(force_other)

    def shift_positions(column, columns, first):
        for shift in (-1, 0, 1):
            if first and shift == 0:
                continue
            ids = lane_ids(SLOTS)
            near_p[column, 1 + shift, 0] = shifted(columns[0], shift)
            near_p[column, 1 + shift, 1] = shifted(columns[1], shift) + float(shift)
            near_p[column, 1 + shift, 2] = shifted(columns[2], shift)
            mass = shifted(columns[3], shift)
            if shift != 0:
                mass = jnp.where(ids == wrapped_lane(shift), 0.0, mass)
            near_p[column, 1 + shift, 3] = mass

    for column in (0, 1):
        shift_positions(column, [near_p[column, 1, f] for f in range(4)], True)

    def density_block(unit, own, near, near_shift, other, first, count, near_first, near_last):
        rows = pl.ds(pl.multiple_of(first, 8), count)
        own_x, own_y, own_z, own_m = (near_p[own, 1, f, rows, :] for f in range(4))

        def step(j, total):
            near_x, near_y, near_z, near_m = (near_p[near, near_shift, f, pl.ds(j, 1), :] for f in range(4))
            dist, spline = spline_of(own_x - near_x, own_y - near_y, own_z - near_z)
            kept[unit, j, rows, :] = spline
            pair = density_pair(dist, spline)
            if other is not None:
                rho_other[other, pl.ds(pl.multiple_of(8 * j, 8), 8), :] += groups_sum(pair * own_m)
            return total + pair * near_m

        total = lax.fori_loop(near_first, near_last, step, jnp.zeros((count, LANES), F32), unroll=DENSITY_UNROLL)
        rho_sum[own, rows, :] += total

    def density_unit(unit, own, near, near_shift, other):
        def part(index, carry):
            density_block(unit, own, near, near_shift, other, index * DENSITY_ROWS, DENSITY_ROWS, 0, SLOTS)
            return carry

        lax.fori_loop(0, SLOTS // DENSITY_ROWS, part, 0)

    def each_same(block, rows):
        for col in range(2):
            for first in range(0, SLOTS, rows):
                block(col, col, col, 1, None, first, rows, first, first + rows)
                if first + rows < SLOTS:
                    block(col, col, col, 1, SAME_ROW[col], first, rows, first + rows, SLOTS)

    def other_sum(sums):
        total = sums[pl.ds(0, SLOTS, stride=8), :]
        for part in range(1, 8):
            total = total + sums[pl.ds(part, SLOTS, stride=8), :]
        return total

    def density_other(slot):
        shift = OTHERS[slot][1]
        back = other_sum(rho_other.at[slot])
        if shift != 0:
            back = jnp.where(lane_ids(SLOTS) == wrapped_lane(shift), 0.0, back)
        return shifted(back, -shift)

    each_same(density_block, FORCE_ROWS)
    density_unit(2, 0, 0, 2, 0)
    density_unit(3, 1, 1, 2, 3)

    pos_copy.wait()
    shift_positions(2, [got_p[0] + 2.0] + [got_p[f] for f in range(1, 4)], False)
    lax.fori_loop(0, 3, lambda k, carry: (density_unit(7 + k, 1, 2, k, 4 + k), carry)[1], 0)
    back_d[...] = density_other(4) + density_other(5) + density_other(6)
    back_d_copy = send(8, back_d, got_d, 1, 0)

    lax.fori_loop(0, 3, lambda k, carry: (density_unit(4 + k, 0, 1, k, 1 + k), carry)[1], 0)

    for copy in edge_copies:
        copy.wait()
    left_half = lane_ids(1) < SLOTS

    def edge_rows(edge):
        inside = jnp.where(gy == 0, 0.0, 1.0) if edge == 0 else jnp.where(gy == gy_count - 1, 0.0, 1.0)
        shift = -1.0 if edge == 0 else 1.0
        blocks = []
        for block in range(2):
            rows = []
            for f in range(7):
                if block == 0:
                    row = edge_got[edge, 0, f : f + 1, :]
                else:
                    right = edge_got[edge, 2, f : f + 1, :]
                    left = edge_got[edge, 1, f : f + 1, :]
                    if f == 0:
                        right = right + 2.0
                        left = left - 2.0
                    row = jnp.where(left_half, right, left)
                if f == 1:
                    row = row + shift
                if f == 3:
                    row = row * inside
                rows.append(row)
            blocks.append(rows)
        return blocks

    def edge_lane(edge):
        return 0 if edge == 0 else LANES - 1

    for edge in range(2):
        lane = edge_lane(edge)
        blocks = edge_rows(edge)
        for col in range(2):
            own_x, own_y, own_z = (near_p[col, 1, f][:, lane : lane + 1] for f in range(3))
            total = jnp.zeros((SLOTS, LANES), F32)
            for rows in blocks:
                dist, spline = spline_of(own_x - rows[0], own_y - rows[1], own_z - rows[2])
                total = total + density_pair(dist, spline) * rows[3]
            summed = jnp.sum(total, axis=1, keepdims=True)
            rho_sum[col] += jnp.where(lane_ids(SLOTS) == lane, summed, 0.0)

    for col in range(2):
        rho = rho_sum[col]
        for slot, (target, _) in enumerate(OTHERS):
            if target == col:
                rho = rho + density_other(slot)
        if col == 0:
            back_d_copy.wait()
            rho = rho + got_d[...]
        occupied = near_p[col, 1, 3] > 0.0
        rho = (4.0 * KERNEL_NORM) * rho
        rho_out[pl.ds(col, SLOTS, stride=2), :] = jnp.where(occupied, rho, 0.0)
        near_r[col, 1, 0] = jnp.where(occupied, rho, 1.0)

    rho_copy = send(9, near_r.at[0, 1, 0], got_r, -1, 0)
    own_rho = [[near_r[col, 1, 0]] for col in range(2)]
    for edge, lane in ((0, 0), (1, LANES - 1)):
        edge_rho[edge] = edge_pack(own_rho, lane)
    edge_rho_copies = []
    for edge, step_y in ((0, -1), (1, 1)):
        for which, step_x in enumerate((0, 1, -1)):
            edge_rho_copies.append(
                send(10 + edge * 3 + which, edge_rho.at[edge], edge_rho_got.at[1 - edge, which], step_x, step_y)
            )

    def shift_rest(column, velocity, rho, first):
        for shift in (-1, 0, 1):
            if not (first and shift == 0):
                for f in range(3):
                    near_v[column, 1 + shift, f] = shifted(velocity[f], shift)
                near_r[column, 1 + shift, 0] = shifted(rho, shift)
            near_r[column, 1 + shift, 1] = pressure_term(shifted(rho, shift))

    for column in (0, 1):
        shift_rest(column, [near_v[column, 1, f] for f in range(3)], near_r[column, 1, 0], True)

    def force_block(unit, own_col, near_col, near_shift, other, first, count, near_first, near_last):
        rows = pl.ds(pl.multiple_of(first, 8), count)
        own = (
            [near_p[own_col, 1, f, rows, :] for f in range(4)]
            + [near_v[own_col, 1, f, rows, :] for f in range(3)]
            + [near_r[own_col, 1, f, rows, :] for f in range(2)]
        )

        def step(j, totals):
            row = pl.ds(j, 1)
            near = (
                [near_p[near_col, near_shift, f, row, :] for f in range(4)]
                + [near_v[near_col, near_shift, f, row, :] for f in range(3)]
                + [near_r[near_col, near_shift, f, row, :] for f in range(2)]
            )
            spline = kept[unit, j, rows, :]
            sep = [own[f] - near[f] for f in range(3)]
            dist = 1.0 - spline
            weight = strength_of(own, near, sep, dist * dist) * (spline * spline * spline) * near[3]
            if other is not None:
                weight = weight * own[3]
            terms = [weight * sep[f] for f in range(3)]
            if other is not None:
                for f in range(3):
                    force_other[f, other, pl.ds(pl.multiple_of(8 * j, 8), 8), :] += groups_sum(terms[f])
            return tuple(totals[f] + terms[f] for f in range(3))

        zeros = tuple(jnp.zeros((count, LANES), F32) for _ in range(3))
        totals = lax.fori_loop(near_first, near_last, step, zeros, unroll=FORCE_UNROLL)
        target = force_one if other is None else force_sum
        for f in range(3):
            target[own_col, f, rows, :] += totals[f]

    def force_unit(unit, own, near, near_shift, other):
        def part(index, carry):
            force_block(unit, own, near, near_shift, other, index * FORCE_ROWS, FORCE_ROWS, 0, SLOTS)
            return carry

        lax.fori_loop(0, SLOTS // FORCE_ROWS, part, 0)

    def force_other_sum(f, slot):
        return shifted(other_sum(force_other.at[f, slot]), -OTHERS[slot][1])

    force_unit(2, 0, 0, 2, 0)
    force_unit(3, 1, 1, 2, 3)
    each_same(force_block, FORCE_ROWS)

    vel_copy.wait()
    rho_copy.wait()
    shift_rest(2, [got_v[f] for f in range(3)], got_r[...], False)
    lax.fori_loop(0, 3, lambda k, carry: (force_unit(7 + k, 1, 2, k, 4 + k), carry)[1], 0)
    for f in range(3):
        back_f[f] = force_other_sum(f, 4) + force_other_sum(f, 5) + force_other_sum(f, 6)
    back_f_copy = send(16, back_f, got_f, 1, 0)

    lax.fori_loop(0, 3, lambda k, carry: (force_unit(4 + k, 0, 1, k, 1 + k), carry)[1], 0)

    for copy in edge_rho_copies:
        copy.wait()
    for edge in range(2):
        lane = edge_lane(edge)
        blocks = edge_rows(edge)
        for block in range(2):
            if block == 0:
                rho = edge_rho_got[edge, 0, 0:1, :]
            else:
                rho = jnp.where(left_half, edge_rho_got[edge, 2, 0:1, :], edge_rho_got[edge, 1, 0:1, :])
            blocks[block] = blocks[block] + [rho, pressure_term(rho)]
        for col in range(2):
            own = (
                [near_p[col, 1, f][:, lane : lane + 1] for f in range(4)]
                + [near_v[col, 1, f][:, lane : lane + 1] for f in range(3)]
                + [near_r[col, 1, f][:, lane : lane + 1] for f in range(2)]
            )
            totals = [jnp.zeros((SLOTS, LANES), F32) for _ in range(3)]
            for near in blocks:
                sep = [own[f] - near[f] for f in range(3)]
                dist, spline = spline_of(*sep)
                weight = strength_of(own, near, sep, dist * dist) * (spline * spline * spline) * near[3]
                totals = [totals[f] + weight * sep[f] for f in range(3)]
            for f in range(3):
                summed = jnp.sum(totals[f], axis=1, keepdims=True)
                force_one[col, f] += jnp.where(lane_ids(SLOTS) == lane, summed, 0.0)

    for col in (1, 0):
        rows = pl.ds(col, SLOTS, stride=2)
        mass = near_p[col, 1, 3]
        occupied = mass > 0.0
        per_mass = 1.0 / jnp.where(occupied, mass, 1.0)
        row_id = (gy * LANES + lane_ids(SLOTS)).astype(F32)
        height = row_id + near_p[col, 1, 1]
        near_floor = jnp.maximum(1.0 - 2.0 * height, 0.0)
        near_ceiling = jnp.maximum(1.0 - 2.0 * (float(LANES * gy_count) - height), 0.0)
        push = WALL_STIFFNESS * (near_floor * near_floor - near_ceiling * near_ceiling)
        if col == 0:
            back_f_copy.wait()
        for f in range(3):
            both = force_sum[col, f]
            for slot, (target, _) in enumerate(OTHERS):
                if target == col:
                    both = both - force_other_sum(f, slot)
            if col == 0:
                both = both - got_f[f]
            force = (20.0 * KERNEL_NORM) * (both * per_mass + force_one[col, f])
            if f == 1:
                force = force + push
            acc_out[f, rows, :] = jnp.where(occupied, force, 0.0)


def on_device(gx_count, gy_count, position, velocity, particle_mass, counts):
    vmem = pl.BlockSpec(memory_space=pltpu.VMEM)
    column = (SLOTS, LANES)
    others = len(OTHERS)
    rho, acceleration = pl.pallas_call(
        functools.partial(kernel, gx_count, gy_count),
        out_shape=(
            jax.ShapeDtypeStruct((2 * SLOTS, LANES), F32),
            jax.ShapeDtypeStruct((3, 2 * SLOTS, LANES), F32),
        ),
        in_specs=[vmem] * 4,
        out_specs=(vmem, vmem),
        scratch_shapes=[
            pltpu.VMEM((3, 3, 4) + column, F32),
            pltpu.VMEM((3, 3, 3) + column, F32),
            pltpu.VMEM((3, 3, 2) + column, F32),
            pltpu.VMEM((4,) + column, F32),
            pltpu.VMEM((3,) + column, F32),
            pltpu.VMEM(column, F32),
            pltpu.VMEM(column, F32),
            pltpu.VMEM(column, F32),
            pltpu.VMEM((3,) + column, F32),
            pltpu.VMEM((3,) + column, F32),
            pltpu.VMEM((2, 8, LANES), F32),
            pltpu.VMEM((2, 3, 8, LANES), F32),
            pltpu.VMEM((2, 8, LANES), F32),
            pltpu.VMEM((2, 3, 8, LANES), F32),
            pltpu.VMEM((UNITS, SLOTS) + column, F32),
            pltpu.VMEM((2,) + column, F32),
            pltpu.VMEM((others, 8 * SLOTS, LANES), F32),
            pltpu.VMEM((2, 3) + column, F32),
            pltpu.VMEM((2, 3) + column, F32),
            pltpu.VMEM((3, others, 8 * SLOTS, LANES), F32),
            pltpu.SemaphoreType.DMA((17,)),
            pltpu.SemaphoreType.DMA((17,)),
        ],
        compiler_params=pltpu.CompilerParams(
            collective_id=0, has_side_effects=True, vmem_limit_bytes=52 * 1024 * 1024
        ),
        cost_estimate=pl.CostEstimate(flops=400_000_000, bytes_accessed=2_000_000, transcendentals=30_000_000),
    )(
        position.reshape(3, 2 * SLOTS, LANES),
        velocity.reshape(3, 2 * SLOTS, LANES),
        particle_mass.reshape(2 * SLOTS, LANES),
        counts,
    )
    return rho.reshape(SLOTS, 2, LANES), acceleration.reshape(3, SLOTS, 2, LANES)


def solution(mesh):
    in_specs = (
        P(None, None, "gx", "gy"),
        P(None, None, "gx", "gy"),
        P(None, "gx", "gy"),
        P("gx", "gy"),
    )
    out_specs = (P(None, "gx", "gy"), P(None, None, "gx", "gy"))
    step = functools.partial(on_device, mesh.shape["gx"], mesh.shape["gy"])
    return jax.shard_map(step, mesh=mesh, in_specs=in_specs, out_specs=out_specs, check_vma=False)
```

```python
import functools

import jax
import jax.numpy as jnp
from jax import lax
from jax.experimental import pallas as pl
from jax.experimental.pallas import tpu as pltpu
from jax.sharding import PartitionSpec as P

MESH = pl.DeviceIdType.MESH
F32 = jnp.float32
KERNEL_NORM = 21.0 / (2.0 * 3.141592653589793)
REST_DENSITY = 0.5
VISCOSITY = 0.5
SMOOTHING = 0.5
WALL_STIFFNESS = 4.0
TINY = 1e-30
SLOTS = 64
LANES = 128

OTHERS = ((0, 1), (1, -1), (1, 0), (1, 1), (2, -1), (2, 0), (2, 1), (0, 0))
SAME_ROW = (7, 2)
INNER = 5
OUTER = 5
SAME = 8
UNITS = 10
SAME_ROWS = 16
JOINT_ROWS = 16
JOINT_UNROLL = 16
OUTER_ROWS = 32
OUTER_UNROLL = 16
FORCE_ROWS = 16
FORCE_UNROLL = 16
BEFORE_SEND = 3
BEFORE_PLACES = (5, 3)
BEFORE_DENSITY = (1, 0)
BEFORE_FORCE = (4, 0)
EPS = 0.01 * SMOOTHING * SMOOTHING
PACE = 2.0 * VISCOSITY * SMOOTHING


def pressure_term(rho):
    return (rho - REST_DENSITY) / (rho * rho)


def spline_of(sep):
    dist_sq = jnp.maximum(sep[0] * sep[0] + sep[1] * sep[1] + sep[2] * sep[2], TINY)
    dist = dist_sq * lax.rsqrt(dist_sq)
    return dist_sq, dist, jnp.maximum(1.0 - dist, 0.0)


def approach_of(own, near, sep, dist_sq):
    closing = (near[4] - own[4]) * sep[0] + (near[5] - own[5]) * sep[1] + (near[6] - own[6]) * sep[2]
    return jnp.maximum(closing, 0.0) / (dist_sq + EPS)


def lane_ids(rows):
    return lax.broadcasted_iota(jnp.int32, (rows, LANES), 1)


def shifted(cells, shift):
    return cells if shift == 0 else pltpu.roll(cells, (-shift) % LANES, 1)


def wrapped_lane(shift):
    return LANES - 1 if shift > 0 else 0


def groups_sum(cells):
    total = cells[0:8]
    for first in range(8, cells.shape[0], 8):
        total = total + cells[first : first + 8]
    return total


def other_rows(j):
    return pl.ds(pl.multiple_of(8 * j, 8), 8)


def kernel(
    gx_count, gy_count,
    pos_hbm, vel_hbm, mass_hbm, counts_hbm, rho_out, acc_out,
    pos_ref, vel_ref, mass_ref, counts_ref,
    near_p, near_v, near_r, got_p, got_v, got_r, back_d, got_d, back_f, got_f,
    edge_own, edge_got, edge_rho, edge_rho_got,
    kept_a, kept_b, rho_sum, rho_other, force_sum, force_other, send_sem, recv_sem, load_sem,
):
    gx = lax.axis_index("gx")
    gy = lax.axis_index("gy")
    early = lax.rem(gx, 2) == 0

    def steps(pair):
        return jnp.where(early, pair[0], pair[1])

    def place(step_x, step_y):
        return (lax.rem(gx + step_x + gx_count, gx_count), lax.rem(gy + step_y + gy_count, gy_count))

    barrier = pltpu.get_barrier_semaphore()
    for step_x in (-1, 0, 1):
        for step_y in (-1, 0, 1):
            if step_x != 0 or step_y != 0:
                pl.semaphore_signal(barrier, inc=1, device_id=place(step_x, step_y), device_id_type=MESH)

    loads = []
    for index, (source, target) in enumerate(
        ((pos_hbm, pos_ref), (counts_hbm, counts_ref), (mass_hbm, mass_ref), (vel_hbm, vel_ref))
    ):
        load = pltpu.make_async_copy(source, target, load_sem.at[index])
        load.start()
        loads.append(load)

    rho_sum[...] = jnp.zeros_like(rho_sum)
    rho_other[...] = jnp.zeros_like(rho_other)
    for load in loads[0:3]:
        load.wait()

    for col in range(2):
        rows = pl.ds(col, SLOTS, stride=2)
        slot = lax.broadcasted_iota(jnp.int32, (SLOTS, LANES), 0)
        occupied = slot < counts_ref[col : col + 1, :]
        near_p[col, 1, 0] = pos_ref[0, rows, :] + float(col)
        near_p[col, 1, 1] = pos_ref[1, rows, :]
        near_p[col, 1, 2] = pos_ref[2, rows, :]
        near_p[col, 1, 3] = jnp.where(occupied, mass_ref[rows, :], 0.0)
    loads[3].wait()
    for col in range(2):
        rows = pl.ds(col, SLOTS, stride=2)
        for axis in range(3):
            near_v[col, 1, axis] = PACE * vel_ref[axis, rows, :]

    def copy_of(index, source, target, step_x, step_y):
        return pltpu.make_async_remote_copy(
            src_ref=source, dst_ref=target, send_sem=send_sem.at[index], recv_sem=recv_sem.at[index],
            device_id=place(step_x, step_y), device_id_type=MESH,
        )

    def send(*args):
        copy = copy_of(*args)
        copy.start()
        return copy

    def edge_pack(fields, lane):
        ids = lane_ids(SLOTS)
        halves = []
        for col in range(2):
            pack = jnp.zeros((SLOTS, LANES), F32)
            for index, field in enumerate(fields[col]):
                pack = jnp.where(ids == index, field[:, lane : lane + 1], pack)
            halves.append(pack)
        return jnp.concatenate(halves, axis=0).T[0:8, :]

    def edge_sends(first, source, target):
        return [
            copy_of(first + edge * 3 + which, source.at[edge], target.at[1 - edge, which], step_x, step_y)
            for edge, step_y in ((0, -1), (1, 1))
            for which, step_x in enumerate((0, 1, -1))
        ]

    own_fields = [
        [near_p[col, 1, f] for f in range(4)] + [near_v[col, 1, f] for f in range(3)] for col in range(2)
    ]

    pos_copy = copy_of(0, near_p.at[1, 1], got_p, 1, 0)
    edge_copies = edge_sends(2, edge_own, edge_got)

    def exchange():
        pl.semaphore_wait(barrier, 8)
        pos_copy.start()
        for edge, lane in ((0, 0), (1, LANES - 1)):
            edge_own[edge] = edge_pack(own_fields, lane)
        for copy in edge_copies:
            copy.start()

    pl.when(jnp.logical_not(early))(exchange)

    def shift_positions(column, columns, first):
        for shift in (-1, 0, 1):
            if first and shift == 0:
                continue
            near_p[column, 1 + shift, 0] = shifted(columns[0], shift)
            near_p[column, 1 + shift, 1] = shifted(columns[1], shift) + float(shift)
            near_p[column, 1 + shift, 2] = shifted(columns[2], shift)
            mass = shifted(columns[3], shift)
            if shift != 0:
                mass = jnp.where(lane_ids(SLOTS) == wrapped_lane(shift), 0.0, mass)
            near_p[column, 1 + shift, 3] = mass

    def shift_velocities(column, columns, first):
        for shift in (-1, 0, 1):
            if not (first and shift == 0):
                for f in range(3):
                    near_v[column, 1 + shift, f] = shifted(columns[f], shift)

    for column in (0, 1):
        shift_positions(column, [near_p[column, 1, f] for f in range(4)], True)
        shift_velocities(column, [near_v[column, 1, f] for f in range(3)], True)

    def fields_of(refs, column, shift, rows):
        return [ref[column, shift, f, rows, :] for ref, count in refs for f in range(count)]

    places = ((near_p, 4),)
    moving = ((near_p, 4), (near_v, 3))

    def pair_block(unit, own_col, near_col, near_shift, other, first, count, near_first, near_count, joint, unroll):
        rows = pl.ds(pl.multiple_of(first, 8), count)
        refs = moving if joint else places
        own = fields_of(refs, own_col, 1, rows)

        def step(index, total):
            j = near_first + index
            near = fields_of(refs, near_col, near_shift, pl.ds(j, 1))
            sep = [own[f] - near[f] for f in range(3)]
            dist_sq, dist, spline = spline_of(sep)
            spline_sq = spline * spline
            both = own[3] * near[3]
            if joint:
                slope = spline_sq * spline * both
                pair = slope * (spline * (dist + 0.25))
                kept_a[unit, j, rows, :] = slope
                kept_b[unit, j, rows, :] = slope * approach_of(own, near, sep, dist_sq)
            else:
                pair = spline_sq * spline_sq * (dist + 0.25) * both
                kept_a[unit, j, rows, :] = spline
            if other is not None:
                rho_other[other, other_rows(j), :] += groups_sum(pair)
            return total + pair

        total = lax.fori_loop(0, near_count, step, jnp.zeros((count, LANES), F32), unroll=unroll)
        rho_sum[own_col, rows, :] += total

    def joint_block(unit, own, near, near_shift, other, first, count, near_first, near_count):
        pair_block(unit, own, near, near_shift, other, first, count, near_first, near_count, True, JOINT_UNROLL)

    def late_block(unit, own_col, near_col, near_shift, first, count):
        rows = pl.ds(pl.multiple_of(first, 8), count)
        own = fields_of(moving, own_col, 1, rows)

        def step(j, carry):
            near = fields_of(moving, near_col, near_shift, pl.ds(j, 1))
            sep = [own[f] - near[f] for f in range(3)]
            spline = kept_a[unit, j, rows, :]
            dist = 1.0 - spline
            slope = spline * spline * spline * (own[3] * near[3])
            kept_a[unit, j, rows, :] = slope
            kept_b[unit, j, rows, :] = slope * approach_of(own, near, sep, dist * dist)
            return carry

        lax.fori_loop(0, SLOTS, step, 0, unroll=JOINT_UNROLL)

    def each_part(rows, block, *args):
        def part(index, carry):
            block(*args, index * rows, rows)
            return carry

        lax.fori_loop(0, SLOTS // rows, part, 0)

    def same_cells(first_col, last_col, block):
        def in_part(part, col):
            first = SAME_ROWS * part
            block(SAME + col, col, col, 1, None, first, SAME_ROWS, first, SAME_ROWS)
            return col

        def in_pair(pair, col):
            part = jnp.where(pair < 3, 0, jnp.where(pair < 5, 1, 2))
            near = pair + 1 - jnp.where(pair < 3, 0, 2) - jnp.where(pair < 5, 0, 1)
            other = jnp.where(col == 0, SAME_ROW[0], SAME_ROW[1])
            block(SAME + col, col, col, 1, other, SAME_ROWS * part, SAME_ROWS, SAME_ROWS * near, SAME_ROWS)
            return col

        def column(col, carry):
            lax.fori_loop(0, SLOTS // SAME_ROWS, in_part, col)
            lax.fori_loop(0, 6, in_pair, col)
            return carry

        lax.fori_loop(first_col, last_col, column, 0)

    def inner_place(k):
        own = jnp.where(k == 1, 1, 0)
        near = jnp.where(k == 0, 0, 1)
        shift = jnp.where(k < 2, 2, k - 2)
        other = jnp.where(k == 0, 0, jnp.where(k == 1, 3, k - 1))
        return own, near, shift, other

    def inner_units(first, last, rows, block):
        def unit(k, carry):
            each_part(rows, lambda *args: block(*args, 0, SLOTS), k, *inner_place(k))
            return carry

        lax.fori_loop(first, last, unit, 0)

    def outer_units(first, last, rows, block):
        def unit(k, carry):
            each_part(rows, block, OUTER + k, 0, 2, k, 4 + k)
            return carry

        lax.fori_loop(first, last, unit, 0)

    def other_sum(sums):
        total = sums[pl.ds(0, SLOTS, stride=8), :]
        for part in range(1, 8):
            total = total + sums[pl.ds(part, SLOTS, stride=8), :]
        return total

    def others_of(sums, column):
        total = None
        for slot, (target, shift) in enumerate(OTHERS):
            if target == column:
                back = shifted(other_sum(sums.at[slot]), -shift)
                total = back if total is None else total + back
        return total

    vel_copy = copy_of(1, near_v.at[1, 1], got_v, 1, 0)

    same_cells(0, 2, joint_block)
    inner_units(0, 1, JOINT_ROWS, joint_block)
    pl.when(jnp.logical_not(early))(vel_copy.start)
    sent = steps((BEFORE_SEND, 1))
    inner_units(1, sent, JOINT_ROWS, joint_block)
    pl.when(early)(exchange)
    ahead = steps(BEFORE_PLACES)
    inner_units(sent, ahead, JOINT_ROWS, joint_block)

    pl.when(early)(vel_copy.start)
    pos_copy.wait()
    shift_positions(2, [got_p[0] - 2.0] + [got_p[f] for f in range(1, 4)], False)
    outer_units(0, 3, OUTER_ROWS, lambda *args: pair_block(*args, 0, SLOTS, False, OUTER_UNROLL))
    back_d[...] = others_of(rho_other, 2)
    back_d_copy = send(8, back_d, got_d, -1, 0)

    inner_units(ahead, INNER, JOINT_ROWS, joint_block)

    for copy in edge_copies:
        copy.wait()
    left_half = lane_ids(1) < SLOTS

    def edge_rows(edge):
        inside = jnp.where(gy == 0, 0.0, 1.0) if edge == 0 else jnp.where(gy == gy_count - 1, 0.0, 1.0)
        shift = -1.0 if edge == 0 else 1.0
        blocks = []
        for block in range(2):
            rows = []
            for f in range(7):
                if block == 0:
                    row = edge_got[edge, 0, f : f + 1, :]
                else:
                    right = edge_got[edge, 2, f : f + 1, :]
                    left = edge_got[edge, 1, f : f + 1, :]
                    if f == 0:
                        right = right + 2.0
                        left = left - 2.0
                    row = jnp.where(left_half, right, left)
                if f == 1:
                    row = row + shift
                if f == 3:
                    row = row * inside
                rows.append(row)
            blocks.append(rows)
        return blocks

    def edge_lane(edge):
        return 0 if edge == 0 else LANES - 1

    def at_edge(total, col, lane):
        summed = jnp.sum(total, axis=1, keepdims=True) * near_p[col, 1, 3]
        return jnp.where(lane_ids(SLOTS) == lane, summed, 0.0)

    for edge in range(2):
        lane = edge_lane(edge)
        blocks = edge_rows(edge)
        for col in range(2):
            own = [near_p[col, 1, f][:, lane : lane + 1] for f in range(3)]
            total = jnp.zeros((SLOTS, LANES), F32)
            for near in blocks:
                _, dist, spline = spline_of([own[f] - near[f] for f in range(3)])
                spline_sq = spline * spline
                total = total + spline_sq * spline_sq * (dist + 0.25) * near[3]
            rho_sum[col] += at_edge(total, col, lane)

    def shift_densities(column, rho, first):
        for shift in (-1, 0, 1):
            if not (first and shift == 0):
                near_r[column, 1 + shift, 0] = shifted(rho, shift)
            near_r[column, 1 + shift, 1] = pressure_term(shifted(rho, shift))

    def occupied_of(col):
        mass = near_p[col, 1, 3]
        occupied = mass > 0.0
        return occupied, 1.0 / jnp.where(occupied, mass, 1.0)

    def finish_density(col, more):
        occupied, per_mass = occupied_of(col)
        rho = rho_sum[col] + others_of(rho_other, col)
        if more is not None:
            rho = rho + more
        rho = (4.0 * KERNEL_NORM) * rho * per_mass
        rho_out[pl.ds(col, SLOTS, stride=2), :] = jnp.where(occupied, rho, 0.0)
        near_r[col, 1, 0] = jnp.where(occupied, rho, 1.0)

    force_sum[...] = jnp.zeros_like(force_sum)
    force_other[...] = jnp.zeros_like(force_other)

    def force_block(unit, own_col, near_col, near_shift, other, first, count, near_first, near_count):
        rows = pl.ds(pl.multiple_of(first, 8), count)
        own = [near_p[own_col, 1, f, rows, :] for f in range(3)] + [near_r[own_col, 1, f, rows, :] for f in range(2)]

        def step(index, totals):
            j = near_first + index
            row = pl.ds(j, 1)
            near = [near_p[near_col, near_shift, f, row, :] for f in range(3)]
            near += [near_r[near_col, near_shift, f, row, :] for f in range(2)]
            weight = kept_a[unit, j, rows, :] * (own[4] + near[4])
            weight = weight + kept_b[unit, j, rows, :] / (own[3] + near[3])
            terms = [weight * (own[f] - near[f]) for f in range(3)]
            if other is not None:
                for f in range(3):
                    force_other[f, other, other_rows(j), :] += groups_sum(terms[f])
            return tuple(totals[f] + terms[f] for f in range(3))

        zeros = tuple(jnp.zeros((count, LANES), F32) for _ in range(3))
        totals = lax.fori_loop(0, near_count, step, zeros, unroll=FORCE_UNROLL)
        for f in range(3):
            force_sum[own_col, f, rows, :] += totals[f]

    def late_units(first, last):
        outer_units(
            first, last, JOINT_ROWS,
            lambda unit, own, near, shift, other, start, count: late_block(unit, own, near, shift, start, count),
        )

    finish_density(0, None)
    shift_densities(0, near_r[0, 1, 0], True)
    vel_copy.wait()
    shift_velocities(2, [got_v[f] for f in range(3)], False)
    done = steps(BEFORE_DENSITY)
    one = steps((1, 0))
    same_cells(0, one, force_block)
    inner_units(0, one, FORCE_ROWS, force_block)
    late_units(0, done)

    back_d_copy.wait()
    finish_density(1, got_d[...])
    rho_copy = send(9, near_r.at[1, 1, 0], got_r, 1, 0)
    own_rho = [[near_r[col, 1, 0]] for col in range(2)]
    for edge, lane in ((0, 0), (1, LANES - 1)):
        edge_rho[edge] = edge_pack(own_rho, lane)
    edge_rho_copies = edge_sends(10, edge_rho, edge_rho_got)
    for copy in edge_rho_copies:
        copy.start()
    shift_densities(1, near_r[1, 1, 0], True)

    late_units(done, 3)
    two = steps((2, 0))
    ahead = steps(BEFORE_FORCE)
    same_cells(one, two, force_block)
    inner_units(one, ahead, FORCE_ROWS, force_block)

    rho_copy.wait()
    shift_densities(2, got_r[...], False)
    outer_units(0, 3, FORCE_ROWS, lambda *args: force_block(*args, 0, SLOTS))
    for f in range(3):
        back_f[f] = others_of(force_other.at[f], 2)
    back_f_copy = send(16, back_f, got_f, -1, 0)

    same_cells(two, 2, force_block)
    inner_units(ahead, INNER, FORCE_ROWS, force_block)

    for copy in edge_rho_copies:
        copy.wait()
    for edge in range(2):
        lane = edge_lane(edge)
        blocks = edge_rows(edge)
        for block in range(2):
            if block == 0:
                rho = edge_rho_got[edge, 0, 0:1, :]
            else:
                rho = jnp.where(left_half, edge_rho_got[edge, 2, 0:1, :], edge_rho_got[edge, 1, 0:1, :])
            blocks[block] = blocks[block] + [rho, pressure_term(rho)]
        for col in range(2):
            own = [ref[col, 1, f][:, lane : lane + 1] for ref, n in ((near_p, 4), (near_v, 3), (near_r, 2)) for f in range(n)]
            totals = [jnp.zeros((SLOTS, LANES), F32) for _ in range(3)]
            for near in blocks:
                sep = [own[f] - near[f] for f in range(3)]
                dist_sq, _, spline = spline_of(sep)
                strength = own[8] + near[8] + approach_of(own, near, sep, dist_sq) / (own[7] + near[7])
                weight = strength * (spline * spline * spline) * near[3]
                totals = [totals[f] + weight * sep[f] for f in range(3)]
            for f in range(3):
                force_sum[col, f] += at_edge(totals[f], col, lane)

    for col in (0, 1):
        rows = pl.ds(col, SLOTS, stride=2)
        occupied, per_mass = occupied_of(col)
        row_id = (gy * LANES + lane_ids(SLOTS)).astype(F32)
        height = row_id + near_p[col, 1, 1]
        near_floor = jnp.maximum(1.0 - 2.0 * height, 0.0)
        near_ceiling = jnp.maximum(1.0 - 2.0 * (float(LANES * gy_count) - height), 0.0)
        push = WALL_STIFFNESS * (near_floor * near_floor - near_ceiling * near_ceiling)
        sums = [force_sum[col, f] - others_of(force_other.at[f], col) for f in range(3)]
        if col == 1:
            back_f_copy.wait()
            sums = [sums[f] - got_f[f] for f in range(3)]
        for f in range(3):
            force = (20.0 * KERNEL_NORM) * sums[f] * per_mass
            if f == 1:
                force = force + push
            acc_out[f, rows, :] = jnp.where(occupied, force, 0.0)


def on_device(gx_count, gy_count, position, velocity, particle_mass, counts):
    vmem = pl.BlockSpec(memory_space=pltpu.VMEM)
    anywhere = pl.BlockSpec(memory_space=pl.ANY)
    column = (SLOTS, LANES)
    others = len(OTHERS)
    rho, acceleration = pl.pallas_call(
        functools.partial(kernel, gx_count, gy_count),
        out_shape=(
            jax.ShapeDtypeStruct((2 * SLOTS, LANES), F32),
            jax.ShapeDtypeStruct((3, 2 * SLOTS, LANES), F32),
        ),
        in_specs=[anywhere] * 4,
        out_specs=(vmem, vmem),
        scratch_shapes=[
            pltpu.VMEM((3, 2 * SLOTS, LANES), F32),
            pltpu.VMEM((3, 2 * SLOTS, LANES), F32),
            pltpu.VMEM((2 * SLOTS, LANES), F32),
            pltpu.VMEM((2, LANES), jnp.int32),
            pltpu.VMEM((3, 3, 4) + column, F32),
            pltpu.VMEM((3, 3, 3) + column, F32),
            pltpu.VMEM((3, 3, 2) + column, F32),
            pltpu.VMEM((4,) + column, F32),
            pltpu.VMEM((3,) + column, F32),
            pltpu.VMEM(column, F32),
            pltpu.VMEM(column, F32),
            pltpu.VMEM(column, F32),
            pltpu.VMEM((3,) + column, F32),
            pltpu.VMEM((3,) + column, F32),
            pltpu.VMEM((2, 8, LANES), F32),
            pltpu.VMEM((2, 3, 8, LANES), F32),
            pltpu.VMEM((2, 8, LANES), F32),
            pltpu.VMEM((2, 3, 8, LANES), F32),
            pltpu.VMEM((UNITS, SLOTS) + column, F32),
            pltpu.VMEM((UNITS, SLOTS) + column, F32),
            pltpu.VMEM((2,) + column, F32),
            pltpu.VMEM((others, 8 * SLOTS, LANES), F32),
            pltpu.VMEM((2, 3) + column, F32),
            pltpu.VMEM((3, others, 8 * SLOTS, LANES), F32),
            pltpu.SemaphoreType.DMA((17,)),
            pltpu.SemaphoreType.DMA((17,)),
            pltpu.SemaphoreType.DMA((4,)),
        ],
        compiler_params=pltpu.CompilerParams(
            collective_id=0, has_side_effects=True, vmem_limit_bytes=58 * 1024 * 1024
        ),
        cost_estimate=pl.CostEstimate(flops=400_000_000, bytes_accessed=2_000_000, transcendentals=30_000_000),
    )(
        position.reshape(3, 2 * SLOTS, LANES),
        velocity.reshape(3, 2 * SLOTS, LANES),
        particle_mass.reshape(2 * SLOTS, LANES),
        counts,
    )
    return rho.reshape(SLOTS, 2, LANES), acceleration.reshape(3, SLOTS, 2, LANES)


def solution(mesh):
    in_specs = (
        P(None, None, "gx", "gy"),
        P(None, None, "gx", "gy"),
        P(None, "gx", "gy"),
        P("gx", "gy"),
    )
    out_specs = (P(None, "gx", "gy"), P(None, None, "gx", "gy"))
    step = functools.partial(on_device, mesh.shape["gx"], mesh.shape["gy"])
    return jax.shard_map(step, mesh=mesh, in_specs=in_specs, out_specs=out_specs, check_vma=False)
```

```python
import functools

import jax
import jax.numpy as jnp
from jax import lax
from jax.experimental import pallas as pl
from jax.experimental.pallas import tpu as pltpu
from jax.sharding import PartitionSpec as P

MESH = pl.DeviceIdType.MESH
F32 = jnp.float32
KERNEL_NORM = 21.0 / (2.0 * 3.141592653589793)
REST_DENSITY = 0.5
VISCOSITY = 0.5
SMOOTHING = 0.5
WALL_STIFFNESS = 4.0
TINY = 1e-30
SLOTS = 64
LANES = 128
HALF = SLOTS // 2

OTHERS = ((0, 1), (1, -1), (1, 0), (1, 1), (2, -1), (2, 0), (2, 1), (0, 0))
SAME_ROW = (7, 2)
INNER = 5
OUTER = 5
SAME = 8
UNITS = 10
SAME_ROWS = 16
JOINT_ROWS = 16
JOINT_UNROLL = 16
OUTER_ROWS = 32
OUTER_UNROLL = 16
FORCE_ROWS = 16
FORCE_UNROLL = 16
BEFORE_SEND = (1, 1)
BEFORE_PLACES = (5, 2)
BEFORE_DENSITY = (1, 0)
BEFORE_FORCE = (5, 0)
EPS = 0.01 * SMOOTHING * SMOOTHING
PACE = 2.0 * VISCOSITY * SMOOTHING


def pressure_term(rho):
    return (rho - REST_DENSITY) / (rho * rho)


def spline_of(sep):
    dist_sq = jnp.maximum(sep[0] * sep[0] + sep[1] * sep[1] + sep[2] * sep[2], TINY)
    dist = dist_sq * lax.rsqrt(dist_sq)
    return dist_sq, dist, jnp.maximum(1.0 - dist, 0.0)


def approach_of(own, near, sep, dist_sq):
    closing = (near[4] - own[4]) * sep[0] + (near[5] - own[5]) * sep[1] + (near[6] - own[6]) * sep[2]
    return jnp.maximum(closing, 0.0) / (dist_sq + EPS)


def lane_ids(rows):
    return lax.broadcasted_iota(jnp.int32, (rows, LANES), 1)


def shifted(cells, shift):
    return cells if shift == 0 else pltpu.roll(cells, (-shift) % LANES, 1)


def wrapped_lane(shift):
    return LANES - 1 if shift > 0 else 0


def groups_sum(cells):
    total = cells[0:8]
    for first in range(8, cells.shape[0], 8):
        total = total + cells[first : first + 8]
    return total


def other_rows(j):
    return pl.ds(pl.multiple_of(8 * j, 8), 8)


def kernel(
    gx_count, gy_count,
    pos_hbm, vel_hbm, mass_hbm, counts_hbm, rho_out, acc_out,
    pos_ref, vel_ref, mass_ref, counts_ref,
    near_p, near_v, near_r, got_p, got_v, got_r, back_d, got_d, back_f, got_f,
    edge_own, edge_got, edge_rho, edge_rho_got,
    kept_a, kept_b, rho_sum, rho_other, force_sum, force_other, send_sem, recv_sem, load_sem, left_sem,
):
    gx = lax.axis_index("gx")
    gy = lax.axis_index("gy")
    early = lax.rem(gx, 2) == 0

    def steps(pair):
        return jnp.where(early, pair[0], pair[1])

    def place(step_x, step_y):
        return (lax.rem(gx + step_x + gx_count, gx_count), lax.rem(gy + step_y + gy_count, gy_count))

    barrier = pltpu.get_barrier_semaphore()
    for step_x, step_y in ((-1, 0), (-1, -1), (-1, 1), (0, -1), (0, 1)):
        pl.semaphore_signal(barrier, inc=1, device_id=place(step_x, step_y), device_id_type=MESH)

    @pl.when(early)
    def _():
        for step_y in (0, -1, 1):
            pl.semaphore_signal(barrier, inc=1, device_id=place(1, step_y), device_id_type=MESH)


    loads = []
    for index, (source, target) in enumerate(
        ((pos_hbm, pos_ref), (counts_hbm, counts_ref), (mass_hbm, mass_ref), (vel_hbm, vel_ref))
    ):
        load = pltpu.make_async_copy(source, target, load_sem.at[index])
        load.start()
        loads.append(load)

    for load in loads[0:3]:
        load.wait()

    def copy_of(index, source, target, step_x, step_y):
        return pltpu.make_async_remote_copy(
            src_ref=source, dst_ref=target, send_sem=send_sem.at[index], recv_sem=recv_sem.at[index],
            device_id=place(step_x, step_y), device_id_type=MESH,
        )

    def send(*args):
        copy = copy_of(*args)
        copy.start()
        return copy

    pos_copy = copy_of(0, near_p.at[1, 1], got_p, 1, 0)

    def enter():
        pl.semaphore_wait(barrier, steps((5, 8)))
        pos_copy.start()

    for col in (1, 0):
        rows = pl.ds(col, SLOTS, stride=2)
        slot = lax.broadcasted_iota(jnp.int32, (SLOTS, LANES), 0)
        occupied = slot < counts_ref[col : col + 1, :]
        near_p[col, 1, 0] = pos_ref[0, rows, :] + float(col)
        near_p[col, 1, 1] = pos_ref[1, rows, :]
        near_p[col, 1, 2] = pos_ref[2, rows, :]
        near_p[col, 1, 3] = jnp.where(occupied, mass_ref[rows, :], 0.0)
        if col == 1:
            pl.when(jnp.logical_not(early))(enter)
    rho_sum[...] = jnp.zeros_like(rho_sum)
    rho_other[...] = jnp.zeros_like(rho_other)
    loads[3].wait()
    for col in range(2):
        rows = pl.ds(col, SLOTS, stride=2)
        for axis in range(3):
            near_v[col, 1, axis] = PACE * vel_ref[axis, rows, :]

    def edge_pack(fields, lane):
        ids = lane_ids(SLOTS)
        halves = []
        for col in range(2):
            pack = jnp.zeros((SLOTS, LANES), F32)
            for index, field in enumerate(fields[col]):
                pack = jnp.where(ids == index, field[:, lane : lane + 1], pack)
            halves.append(pack)
        return jnp.concatenate(halves, axis=0).T[0:8, :]

    def edge_sends(first, source, target):
        return [
            copy_of(first + edge * 3 + which, source.at[edge], target.at[1 - edge, which], step_x, step_y)
            for edge, step_y in ((0, -1), (1, 1))
            for which, step_x in enumerate((0, 1, -1))
        ]

    own_fields = [
        [near_p[col, 1, f] for f in range(4)] + [near_v[col, 1, f] for f in range(3)] for col in range(2)
    ]

    edge_copies = edge_sends(2, edge_own, edge_got)

    def pack_edges():
        for edge, lane in ((0, 0), (1, LANES - 1)):
            edge_own[edge] = edge_pack(own_fields, lane)

    def start_early():
        enter()
        pack_edges()
        for index in (0, 1, 3, 4):
            edge_copies[index].start()

    def start_late():
        for step_y in (0, -1, 1):
            pl.semaphore_signal(left_sem, inc=1, device_id=place(1, step_y), device_id_type=MESH)
        pack_edges()
        for copy in edge_copies:
            copy.start()

    pl.when(jnp.logical_not(early))(start_late)

    def shift_positions(column, columns, first):
        for shift in (-1, 0, 1):
            if first and shift == 0:
                continue
            near_p[column, 1 + shift, 0] = shifted(columns[0], shift)
            near_p[column, 1 + shift, 1] = shifted(columns[1], shift) + float(shift)
            near_p[column, 1 + shift, 2] = shifted(columns[2], shift)
            mass = shifted(columns[3], shift)
            if shift != 0:
                mass = jnp.where(lane_ids(SLOTS) == wrapped_lane(shift), 0.0, mass)
            near_p[column, 1 + shift, 3] = mass

    def shift_velocities(column, columns, first):
        for shift in (-1, 0, 1):
            if not (first and shift == 0):
                for f in range(3):
                    near_v[column, 1 + shift, f] = shifted(columns[f], shift)

    for column in (0, 1):
        shift_positions(column, [near_p[column, 1, f] for f in range(4)], True)
        shift_velocities(column, [near_v[column, 1, f] for f in range(3)], True)

    def fields_of(refs, column, shift, rows):
        return [ref[column, shift, f, rows, :] for ref, count in refs for f in range(count)]

    places = ((near_p, 4),)
    moving = ((near_p, 4), (near_v, 3))

    def pair_block(unit, own_col, near_col, near_shift, other, first, count, near_first, near_count, joint, unroll):
        rows = pl.ds(pl.multiple_of(first, 8), count)
        refs = moving if joint else places
        own = fields_of(refs, own_col, 1, rows)

        def step(index, total):
            j = near_first + index
            near = fields_of(refs, near_col, near_shift, pl.ds(j, 1))
            sep = [own[f] - near[f] for f in range(3)]
            dist_sq, dist, spline = spline_of(sep)
            spline_sq = spline * spline
            both = own[3] * near[3]
            if joint:
                slope = spline_sq * spline * both
                pair = slope * (spline * (dist + 0.25))
                kept_a[unit, j, rows, :] = slope
                kept_b[unit, j, rows, :] = slope * approach_of(own, near, sep, dist_sq)
            else:
                pair = spline_sq * spline_sq * (dist + 0.25) * both
                kept_a[unit, j, rows, :] = spline
            if other is not None:
                rho_other[other, other_rows(j), :] += groups_sum(pair)
            return total + pair

        total = lax.fori_loop(0, near_count, step, jnp.zeros((count, LANES), F32), unroll=unroll)
        rho_sum[own_col, rows, :] += total

    def joint_block(unit, own, near, near_shift, other, first, count, near_first, near_count):
        pair_block(unit, own, near, near_shift, other, first, count, near_first, near_count, True, JOINT_UNROLL)

    def late_block(unit, own_col, near_col, near_shift, first, count):
        rows = pl.ds(pl.multiple_of(first, 8), count)
        own = fields_of(moving, own_col, 1, rows)

        def step(j, carry):
            near = fields_of(moving, near_col, near_shift, pl.ds(j, 1))
            sep = [own[f] - near[f] for f in range(3)]
            spline = kept_a[unit, j, rows, :]
            dist = 1.0 - spline
            slope = spline * spline * spline * (own[3] * near[3])
            kept_a[unit, j, rows, :] = slope
            kept_b[unit, j, rows, :] = slope * approach_of(own, near, sep, dist * dist)
            return carry

        lax.fori_loop(0, SLOTS, step, 0, unroll=JOINT_UNROLL)

    def each_part(rows, block, *args):
        def part(index, carry):
            block(*args, index * rows, rows)
            return carry

        lax.fori_loop(0, SLOTS // rows, part, 0)

    def same_cells(first_col, last_col, block):
        def in_part(part, col):
            first = SAME_ROWS * part
            block(SAME + col, col, col, 1, None, first, SAME_ROWS, first, SAME_ROWS)
            return col

        def in_pair(pair, col):
            part = jnp.where(pair < 3, 0, jnp.where(pair < 5, 1, 2))
            near = pair + 1 - jnp.where(pair < 3, 0, 2) - jnp.where(pair < 5, 0, 1)
            other = jnp.where(col == 0, SAME_ROW[0], SAME_ROW[1])
            block(SAME + col, col, col, 1, other, SAME_ROWS * part, SAME_ROWS, SAME_ROWS * near, SAME_ROWS)
            return col

        def column(col, carry):
            lax.fori_loop(0, SLOTS // SAME_ROWS, in_part, col)
            lax.fori_loop(0, 6, in_pair, col)
            return carry

        lax.fori_loop(first_col, last_col, column, 0)

    def inner_place(k):
        own = jnp.where(k == 1, 1, 0)
        near = jnp.where(k == 0, 0, 1)
        shift = jnp.where(k < 2, 2, k - 2)
        other = jnp.where(k == 0, 0, jnp.where(k == 1, 3, k - 1))
        return own, near, shift, other

    def inner_units(first, last, rows, block):
        def unit(k, carry):
            each_part(rows, lambda *args: block(*args, 0, SLOTS), k, *inner_place(k))
            return carry

        lax.fori_loop(first, last, unit, 0)

    def outer_units(first, last, rows, block):
        def unit(k, carry):
            each_part(rows, block, OUTER + k, 0, 2, k, 4 + k)
            return carry

        lax.fori_loop(first, last, unit, 0)

    def other_sum(sums, first, count):
        total = sums[pl.ds(8 * first, count, stride=8), :]
        for part in range(1, 8):
            total = total + sums[pl.ds(8 * first + part, count, stride=8), :]
        return total

    def others_of(sums, column, first=0, count=SLOTS):
        total = None
        for slot, (target, shift) in enumerate(OTHERS):
            if target == column:
                back = shifted(other_sum(sums.at[slot], first, count), -shift)
                total = back if total is None else total + back
        return total

    vel_copy = copy_of(1, near_v.at[1, 1], got_v, 1, 0)

    same_cells(0, 2, joint_block)
    inner_units(0, 1, JOINT_ROWS, joint_block)
    sent = steps(BEFORE_SEND)
    inner_units(1, sent, JOINT_ROWS, joint_block)
    pl.when(early)(start_early)
    ahead = steps(BEFORE_PLACES)
    inner_units(sent, ahead, JOINT_ROWS, joint_block)

    force_sum[...] = jnp.zeros_like(force_sum)
    force_other[...] = jnp.zeros_like(force_other)
    pos_copy.wait()
    vel_copy.start()

    @pl.when(early)
    def _():
        pl.semaphore_wait(left_sem, 3)
        edge_copies[2].start()
        edge_copies[5].start()

    shift_positions(2, [got_p[0] - 2.0] + [got_p[f] for f in range(1, 4)], False)
    outer_units(0, 3, OUTER_ROWS, lambda *args: pair_block(*args, 0, SLOTS, False, OUTER_UNROLL))
    back_d[...] = others_of(rho_other, 2)
    back_d_copy = send(8, back_d, got_d, -1, 0)

    inner_units(ahead, INNER, JOINT_ROWS, joint_block)

    for copy in edge_copies:
        copy.wait()
    left_half = lane_ids(1) < SLOTS

    def edge_rows(edge):
        inside = jnp.where(gy == 0, 0.0, 1.0) if edge == 0 else jnp.where(gy == gy_count - 1, 0.0, 1.0)
        shift = -1.0 if edge == 0 else 1.0
        blocks = []
        for block in range(2):
            rows = []
            for f in range(7):
                if block == 0:
                    row = edge_got[edge, 0, f : f + 1, :]
                else:
                    right = edge_got[edge, 2, f : f + 1, :]
                    left = edge_got[edge, 1, f : f + 1, :]
                    if f == 0:
                        right = right + 2.0
                        left = left - 2.0
                    row = jnp.where(left_half, right, left)
                if f == 1:
                    row = row + shift
                if f == 3:
                    row = row * inside
                rows.append(row)
            blocks.append(rows)
        return blocks

    def edge_lane(edge):
        return 0 if edge == 0 else LANES - 1

    def at_edge(total, col, lane):
        summed = jnp.sum(total, axis=1, keepdims=True) * near_p[col, 1, 3]
        return jnp.where(lane_ids(SLOTS) == lane, summed, 0.0)

    for edge in range(2):
        lane = edge_lane(edge)
        blocks = edge_rows(edge)
        for col in range(2):
            own = [near_p[col, 1, f][:, lane : lane + 1] for f in range(3)]
            total = jnp.zeros((SLOTS, LANES), F32)
            for near in blocks:
                _, dist, spline = spline_of([own[f] - near[f] for f in range(3)])
                spline_sq = spline * spline
                total = total + spline_sq * spline_sq * (dist + 0.25) * near[3]
            rho_sum[col] += at_edge(total, col, lane)

    def shift_densities(column, rho, first):
        for shift in (-1, 0, 1):
            if not (first and shift == 0):
                near_r[column, 1 + shift, 0] = shifted(rho, shift)
            near_r[column, 1 + shift, 1] = pressure_term(shifted(rho, shift))

    def occupied_of(col):
        mass = near_p[col, 1, 3]
        occupied = mass > 0.0
        return occupied, 1.0 / jnp.where(occupied, mass, 1.0)

    def finish_density(col, more):
        occupied, per_mass = occupied_of(col)
        rho = rho_sum[col] + others_of(rho_other, col)
        if more is not None:
            rho = rho + more
        rho = (4.0 * KERNEL_NORM) * rho * per_mass
        rho_out[pl.ds(col, SLOTS, stride=2), :] = jnp.where(occupied, rho, 0.0)
        near_r[col, 1, 0] = jnp.where(occupied, rho, 1.0)


    def force_block(unit, own_col, near_col, near_shift, other, first, count, near_first, near_count):
        rows = pl.ds(pl.multiple_of(first, 8), count)
        own = [near_p[own_col, 1, f, rows, :] for f in range(3)] + [near_r[own_col, 1, f, rows, :] for f in range(2)]

        def step(index, totals):
            j = near_first + index
            row = pl.ds(j, 1)
            near = [near_p[near_col, near_shift, f, row, :] for f in range(3)]
            near += [near_r[near_col, near_shift, f, row, :] for f in range(2)]
            weight = kept_a[unit, j, rows, :] * (own[4] + near[4])
            weight = weight + kept_b[unit, j, rows, :] / (own[3] + near[3])
            terms = [weight * (own[f] - near[f]) for f in range(3)]
            if other is not None:
                for f in range(3):
                    force_other[f, other, other_rows(j), :] += groups_sum(terms[f])
            return tuple(totals[f] + terms[f] for f in range(3))

        zeros = tuple(jnp.zeros((count, LANES), F32) for _ in range(3))
        totals = lax.fori_loop(0, near_count, step, zeros, unroll=FORCE_UNROLL)
        for f in range(3):
            force_sum[own_col, f, rows, :] += totals[f]

    def late_units(first, last):
        outer_units(
            first, last, JOINT_ROWS,
            lambda unit, own, near, shift, other, start, count: late_block(unit, own, near, shift, start, count),
        )

    finish_density(0, None)
    shift_densities(0, near_r[0, 1, 0], True)
    done = steps(BEFORE_DENSITY)
    one = steps((1, 0))
    same_cells(0, one, force_block)
    inner_units(0, one, FORCE_ROWS, force_block)
    vel_copy.wait()
    shift_velocities(2, [got_v[f] for f in range(3)], False)
    late_units(0, done)

    back_d_copy.wait()
    finish_density(1, got_d[...])
    rho_copy = send(9, near_r.at[1, 1, 0], got_r, 1, 0)
    own_rho = [[near_r[col, 1, 0]] for col in range(2)]
    for edge, lane in ((0, 0), (1, LANES - 1)):
        edge_rho[edge] = edge_pack(own_rho, lane)
    edge_rho_copies = edge_sends(10, edge_rho, edge_rho_got)
    for copy in edge_rho_copies:
        copy.start()
    shift_densities(1, near_r[1, 1, 0], True)

    late_units(done, 3)
    two = steps((2, 0))
    ahead = steps(BEFORE_FORCE)
    same_cells(one, two, force_block)
    inner_units(one, ahead, FORCE_ROWS, force_block)

    rho_copy.wait()
    shift_densities(2, got_r[...], False)
    back_f_copies = []
    for half in range(2):
        first, count = HALF * half, HALF
        outer_units(0, 3, FORCE_ROWS, lambda *args: force_block(*args, first, count))
        for f in range(3):
            back_f[half, f] = others_of(force_other.at[f], 2, first, count)
        back_f_copies.append(send(16 + half, back_f.at[half], got_f.at[half], -1, 0))

    same_cells(two, 2, force_block)
    inner_units(ahead, INNER, FORCE_ROWS, force_block)

    for copy in edge_rho_copies:
        copy.wait()
    for edge in range(2):
        lane = edge_lane(edge)
        blocks = edge_rows(edge)
        for block in range(2):
            if block == 0:
                rho = edge_rho_got[edge, 0, 0:1, :]
            else:
                rho = jnp.where(left_half, edge_rho_got[edge, 2, 0:1, :], edge_rho_got[edge, 1, 0:1, :])
            blocks[block] = blocks[block] + [rho, pressure_term(rho)]
        for col in range(2):
            own = [ref[col, 1, f][:, lane : lane + 1] for ref, n in ((near_p, 4), (near_v, 3), (near_r, 2)) for f in range(n)]
            totals = [jnp.zeros((SLOTS, LANES), F32) for _ in range(3)]
            for near in blocks:
                sep = [own[f] - near[f] for f in range(3)]
                dist_sq, _, spline = spline_of(sep)
                strength = own[8] + near[8] + approach_of(own, near, sep, dist_sq) / (own[7] + near[7])
                weight = strength * (spline * spline * spline) * near[3]
                totals = [totals[f] + weight * sep[f] for f in range(3)]
            for f in range(3):
                force_sum[col, f] += at_edge(totals[f], col, lane)

    for col in (0, 1):
        rows = pl.ds(col, SLOTS, stride=2)
        occupied, per_mass = occupied_of(col)
        row_id = (gy * LANES + lane_ids(SLOTS)).astype(F32)
        height = row_id + near_p[col, 1, 1]
        near_floor = jnp.maximum(1.0 - 2.0 * height, 0.0)
        near_ceiling = jnp.maximum(1.0 - 2.0 * (float(LANES * gy_count) - height), 0.0)
        push = WALL_STIFFNESS * (near_floor * near_floor - near_ceiling * near_ceiling)
        sums = [force_sum[col, f] - others_of(force_other.at[f], col) for f in range(3)]
        if col == 1:
            for copy in back_f_copies:
                copy.wait()
            sums = [sums[f] - jnp.concatenate([got_f[0, f], got_f[1, f]], axis=0) for f in range(3)]
        for f in range(3):
            force = (20.0 * KERNEL_NORM) * sums[f] * per_mass
            if f == 1:
                force = force + push
            acc_out[f, rows, :] = jnp.where(occupied, force, 0.0)


def on_device(gx_count, gy_count, position, velocity, particle_mass, counts):
    vmem = pl.BlockSpec(memory_space=pltpu.VMEM)
    anywhere = pl.BlockSpec(memory_space=pl.ANY)
    column = (SLOTS, LANES)
    others = len(OTHERS)
    rho, acceleration = pl.pallas_call(
        functools.partial(kernel, gx_count, gy_count),
        out_shape=(
            jax.ShapeDtypeStruct((2 * SLOTS, LANES), F32),
            jax.ShapeDtypeStruct((3, 2 * SLOTS, LANES), F32),
        ),
        in_specs=[anywhere] * 4,
        out_specs=(vmem, vmem),
        scratch_shapes=[
            pltpu.VMEM((3, 2 * SLOTS, LANES), F32),
            pltpu.VMEM((3, 2 * SLOTS, LANES), F32),
            pltpu.VMEM((2 * SLOTS, LANES), F32),
            pltpu.VMEM((2, LANES), jnp.int32),
            pltpu.VMEM((3, 3, 4) + column, F32),
            pltpu.VMEM((3, 3, 3) + column, F32),
            pltpu.VMEM((3, 3, 2) + column, F32),
            pltpu.VMEM((4,) + column, F32),
            pltpu.VMEM((3,) + column, F32),
            pltpu.VMEM(column, F32),
            pltpu.VMEM(column, F32),
            pltpu.VMEM(column, F32),
            pltpu.VMEM((2, 3, HALF, LANES), F32),
            pltpu.VMEM((2, 3, HALF, LANES), F32),
            pltpu.VMEM((2, 8, LANES), F32),
            pltpu.VMEM((2, 3, 8, LANES), F32),
            pltpu.VMEM((2, 8, LANES), F32),
            pltpu.VMEM((2, 3, 8, LANES), F32),
            pltpu.VMEM((UNITS, SLOTS) + column, F32),
            pltpu.VMEM((UNITS, SLOTS) + column, F32),
            pltpu.VMEM((2,) + column, F32),
            pltpu.VMEM((others, 8 * SLOTS, LANES), F32),
            pltpu.VMEM((2, 3) + column, F32),
            pltpu.VMEM((3, others, 8 * SLOTS, LANES), F32),
            pltpu.SemaphoreType.DMA((18,)),
            pltpu.SemaphoreType.DMA((18,)),
            pltpu.SemaphoreType.DMA((4,)),
            pltpu.SemaphoreType.REGULAR,
        ],
        compiler_params=pltpu.CompilerParams(
            collective_id=0, has_side_effects=True, vmem_limit_bytes=58 * 1024 * 1024
        ),
        cost_estimate=pl.CostEstimate(flops=400_000_000, bytes_accessed=2_000_000, transcendentals=30_000_000),
    )(
        position.reshape(3, 2 * SLOTS, LANES),
        velocity.reshape(3, 2 * SLOTS, LANES),
        particle_mass.reshape(2 * SLOTS, LANES),
        counts,
    )
    return rho.reshape(SLOTS, 2, LANES), acceleration.reshape(3, SLOTS, 2, LANES)


def solution(mesh):
    in_specs = (
        P(None, None, "gx", "gy"),
        P(None, None, "gx", "gy"),
        P(None, "gx", "gy"),
        P("gx", "gy"),
    )
    out_specs = (P(None, "gx", "gy"), P(None, None, "gx", "gy"))
    step = functools.partial(on_device, mesh.shape["gx"], mesh.shape["gy"])
    return jax.shard_map(step, mesh=mesh, in_specs=in_specs, out_specs=out_specs, check_vma=False)
```

```python
import functools

import jax
import jax.numpy as jnp
from jax import lax
from jax.experimental import pallas as pl
from jax.experimental.pallas import tpu as pltpu
from jax.sharding import PartitionSpec as P

MESH = pl.DeviceIdType.MESH
F32 = jnp.float32
KERNEL_NORM = 21.0 / (2.0 * 3.141592653589793)
REST_DENSITY = 0.5
VISCOSITY = 0.5
SMOOTHING = 0.5
WALL_STIFFNESS = 4.0
TINY = 1e-30
SLOTS = 64
LANES = 128
HALF = SLOTS // 2

OTHERS = ((0, 1), (1, -1), (1, 0), (1, 1), (2, -1), (2, 0), (2, 1), (0, 0))
SAME_ROW = (7, 2)
INNER = 5
OUTER = 5
SAME = 8
UNITS = 10
SAME_ROWS = 16
JOINT_ROWS = 32
JOINT_UNROLL = 16
OUTER_ROWS = 32
OUTER_UNROLL = 16
FORCE_ROWS = 16
FORCE_UNROLL = 16
BEFORE_SEND = (1, 1)
BEFORE_PLACES = (5, 2)
BEFORE_DENSITY = (1, 0)
BEFORE_FORCE = (5, 0)
EPS = 0.01 * SMOOTHING * SMOOTHING
PACE = 2.0 * VISCOSITY * SMOOTHING


def pressure_term(rho):
    return (rho - REST_DENSITY) / (rho * rho)


def spline_of(sep):
    dist_sq = jnp.maximum(sep[0] * sep[0] + sep[1] * sep[1] + sep[2] * sep[2], TINY)
    dist = dist_sq * lax.rsqrt(dist_sq)
    return dist_sq, dist, jnp.maximum(1.0 - dist, 0.0)


def approach_of(own, near, sep, dist_sq):
    closing = (near[4] - own[4]) * sep[0] + (near[5] - own[5]) * sep[1] + (near[6] - own[6]) * sep[2]
    return jnp.maximum(closing, 0.0) / (dist_sq + EPS)


def lane_ids(rows):
    return lax.broadcasted_iota(jnp.int32, (rows, LANES), 1)


def shifted(cells, shift):
    return cells if shift == 0 else pltpu.roll(cells, (-shift) % LANES, 1)


def wrapped_lane(shift):
    return LANES - 1 if shift > 0 else 0


def groups_sum(cells):
    total = cells[0:8]
    for first in range(8, cells.shape[0], 8):
        total = total + cells[first : first + 8]
    return total


def other_rows(j):
    return pl.ds(pl.multiple_of(8 * j, 8), 8)


def kernel(
    gx_count, gy_count,
    pos_hbm, vel_hbm, mass_hbm, counts_hbm, rho_out, acc_out,
    pos_ref, vel_ref, mass_ref, counts_ref,
    near_p, near_v, near_r, got_p, got_v, got_r, back_d, got_d, back_f, got_f,
    edge_own, edge_got, edge_rho, edge_rho_got,
    kept_a, kept_b, rho_sum, rho_other, force_sum, force_other, send_sem, recv_sem, load_sem, left_sem,
):
    gx = lax.axis_index("gx")
    gy = lax.axis_index("gy")
    early = lax.rem(gx, 2) == 0

    def steps(pair):
        return jnp.where(early, pair[0], pair[1])

    def place(step_x, step_y):
        return (lax.rem(gx + step_x + gx_count, gx_count), lax.rem(gy + step_y + gy_count, gy_count))

    barrier = pltpu.get_barrier_semaphore()
    for step_x, step_y in ((-1, 0), (-1, -1), (-1, 1), (0, -1), (0, 1)):
        pl.semaphore_signal(barrier, inc=1, device_id=place(step_x, step_y), device_id_type=MESH)

    @pl.when(early)
    def _():
        for step_y in (0, -1, 1):
            pl.semaphore_signal(barrier, inc=1, device_id=place(1, step_y), device_id_type=MESH)


    loads = []
    for index, (source, target) in enumerate(
        ((pos_hbm, pos_ref), (counts_hbm, counts_ref), (mass_hbm, mass_ref), (vel_hbm, vel_ref))
    ):
        load = pltpu.make_async_copy(source, target, load_sem.at[index])
        load.start()
        loads.append(load)

    for load in loads[0:3]:
        load.wait()

    def copy_of(index, source, target, step_x, step_y):
        return pltpu.make_async_remote_copy(
            src_ref=source, dst_ref=target, send_sem=send_sem.at[index], recv_sem=recv_sem.at[index],
            device_id=place(step_x, step_y), device_id_type=MESH,
        )

    def send(*args):
        copy = copy_of(*args)
        copy.start()
        return copy

    pos_copy = copy_of(0, near_p.at[1, 1], got_p, 1, 0)

    def enter():
        pl.semaphore_wait(barrier, steps((5, 8)))
        pos_copy.start()

    for col in (1, 0):
        rows = pl.ds(col, SLOTS, stride=2)
        slot = lax.broadcasted_iota(jnp.int32, (SLOTS, LANES), 0)
        occupied = slot < counts_ref[col : col + 1, :]
        near_p[col, 1, 0] = pos_ref[0, rows, :] + float(col)
        near_p[col, 1, 1] = pos_ref[1, rows, :]
        near_p[col, 1, 2] = pos_ref[2, rows, :]
        near_p[col, 1, 3] = jnp.where(occupied, mass_ref[rows, :], 0.0)
        if col == 1:
            pl.when(jnp.logical_not(early))(enter)
    rho_sum[...] = jnp.zeros_like(rho_sum)
    rho_other[...] = jnp.zeros_like(rho_other)
    loads[3].wait()
    for col in range(2):
        rows = pl.ds(col, SLOTS, stride=2)
        for axis in range(3):
            near_v[col, 1, axis] = PACE * vel_ref[axis, rows, :]

    def edge_pack(fields, lane):
        ids = lane_ids(SLOTS)
        halves = []
        for col in range(2):
            pack = jnp.zeros((SLOTS, LANES), F32)
            for index, field in enumerate(fields[col]):
                pack = jnp.where(ids == index, field[:, lane : lane + 1], pack)
            halves.append(pack)
        return jnp.concatenate(halves, axis=0).T[0:8, :]

    def edge_sends(first, source, target):
        return [
            copy_of(first + edge * 3 + which, source.at[edge], target.at[1 - edge, which], step_x, step_y)
            for edge, step_y in ((0, -1), (1, 1))
            for which, step_x in enumerate((0, 1, -1))
        ]

    own_fields = [
        [near_p[col, 1, f] for f in range(4)] + [near_v[col, 1, f] for f in range(3)] for col in range(2)
    ]

    edge_copies = edge_sends(2, edge_own, edge_got)

    def pack_edges():
        for edge, lane in ((0, 0), (1, LANES - 1)):
            edge_own[edge] = edge_pack(own_fields, lane)

    def start_early():
        enter()
        pack_edges()
        for index in (0, 1, 3, 4):
            edge_copies[index].start()

    def start_late():
        for step_y in (0, -1, 1):
            pl.semaphore_signal(left_sem, inc=1, device_id=place(1, step_y), device_id_type=MESH)
        pack_edges()
        for copy in edge_copies:
            copy.start()

    pl.when(jnp.logical_not(early))(start_late)

    def shift_positions(column, columns, first):
        for shift in (-1, 0, 1):
            if first and shift == 0:
                continue
            near_p[column, 1 + shift, 0] = shifted(columns[0], shift)
            near_p[column, 1 + shift, 1] = shifted(columns[1], shift) + float(shift)
            near_p[column, 1 + shift, 2] = shifted(columns[2], shift)
            mass = shifted(columns[3], shift)
            if shift != 0:
                mass = jnp.where(lane_ids(SLOTS) == wrapped_lane(shift), 0.0, mass)
            near_p[column, 1 + shift, 3] = mass

    def shift_velocities(column, columns, first):
        for shift in (-1, 0, 1):
            if not (first and shift == 0):
                for f in range(3):
                    near_v[column, 1 + shift, f] = shifted(columns[f], shift)

    for column in (0, 1):
        shift_positions(column, [near_p[column, 1, f] for f in range(4)], True)
        shift_velocities(column, [near_v[column, 1, f] for f in range(3)], True)

    def fields_of(refs, column, shift, rows):
        return [ref[column, shift, f, rows, :] for ref, count in refs for f in range(count)]

    places = ((near_p, 4),)
    moving = ((near_p, 4), (near_v, 3))

    def pair_block(unit, own_col, near_col, near_shift, other, first, count, near_first, near_count, joint, unroll):
        rows = pl.ds(pl.multiple_of(first, 8), count)
        refs = moving if joint else places
        own = fields_of(refs, own_col, 1, rows)

        def step(index, total):
            j = near_first + index
            near = fields_of(refs, near_col, near_shift, pl.ds(j, 1))
            sep = [own[f] - near[f] for f in range(3)]
            dist_sq, dist, spline = spline_of(sep)
            spline_sq = spline * spline
            both = own[3] * near[3]
            if joint:
                slope = spline_sq * spline * both
                pair = slope * (spline * (dist + 0.25))
                kept_a[unit, j, rows, :] = slope
                kept_b[unit, j, rows, :] = slope * approach_of(own, near, sep, dist_sq)
            else:
                pair = spline_sq * spline_sq * (dist + 0.25) * both
                kept_a[unit, j, rows, :] = spline
            if other is not None:
                rho_other[other, other_rows(j), :] += groups_sum(pair)
            return total + pair

        total = lax.fori_loop(0, near_count, step, jnp.zeros((count, LANES), F32), unroll=unroll)
        rho_sum[own_col, rows, :] += total

    def joint_block(unit, own, near, near_shift, other, first, count, near_first, near_count):
        pair_block(unit, own, near, near_shift, other, first, count, near_first, near_count, True, JOINT_UNROLL)

    def late_block(unit, own_col, near_col, near_shift, first, count):
        rows = pl.ds(pl.multiple_of(first, 8), count)
        own = fields_of(moving, own_col, 1, rows)

        def step(j, carry):
            near = fields_of(moving, near_col, near_shift, pl.ds(j, 1))
            sep = [own[f] - near[f] for f in range(3)]
            spline = kept_a[unit, j, rows, :]
            dist = 1.0 - spline
            slope = spline * spline * spline * (own[3] * near[3])
            kept_a[unit, j, rows, :] = slope
            kept_b[unit, j, rows, :] = slope * approach_of(own, near, sep, dist * dist)
            return carry

        lax.fori_loop(0, SLOTS, step, 0, unroll=JOINT_UNROLL)

    def each_part(rows, block, *args):
        def part(index, carry):
            block(*args, index * rows, rows)
            return carry

        lax.fori_loop(0, SLOTS // rows, part, 0)

    def same_cells(first_col, last_col, block):
        def in_part(part, col):
            first = SAME_ROWS * part
            block(SAME + col, col, col, 1, None, first, SAME_ROWS, first, SAME_ROWS)
            return col

        def in_pair(pair, col):
            part = jnp.where(pair < 3, 0, jnp.where(pair < 5, 1, 2))
            near = pair + 1 - jnp.where(pair < 3, 0, 2) - jnp.where(pair < 5, 0, 1)
            other = jnp.where(col == 0, SAME_ROW[0], SAME_ROW[1])
            block(SAME + col, col, col, 1, other, SAME_ROWS * part, SAME_ROWS, SAME_ROWS * near, SAME_ROWS)
            return col

        def column(col, carry):
            lax.fori_loop(0, SLOTS // SAME_ROWS, in_part, col)
            lax.fori_loop(0, 6, in_pair, col)
            return carry

        lax.fori_loop(first_col, last_col, column, 0)

    def inner_place(k):
        own = jnp.where(k == 1, 1, 0)
        near = jnp.where(k == 0, 0, 1)
        shift = jnp.where(k < 2, 2, k - 2)
        other = jnp.where(k == 0, 0, jnp.where(k == 1, 3, k - 1))
        return own, near, shift, other

    def inner_units(first, last, rows, block):
        def unit(k, carry):
            each_part(rows, lambda *args: block(*args, 0, SLOTS), k, *inner_place(k))
            return carry

        lax.fori_loop(first, last, unit, 0)

    def outer_units(first, last, rows, block):
        def unit(k, carry):
            each_part(rows, block, OUTER + k, 0, 2, k, 4 + k)
            return carry

        lax.fori_loop(first, last, unit, 0)

    def other_sum(sums, first, count):
        total = sums[pl.ds(8 * first, count, stride=8), :]
        for part in range(1, 8):
            total = total + sums[pl.ds(8 * first + part, count, stride=8), :]
        return total

    def others_of(sums, column, first=0, count=SLOTS):
        total = None
        for slot, (target, shift) in enumerate(OTHERS):
            if target == column:
                back = shifted(other_sum(sums.at[slot], first, count), -shift)
                total = back if total is None else total + back
        return total

    vel_copy = copy_of(1, near_v.at[1, 1], got_v, 1, 0)

    same_cells(0, 2, joint_block)
    inner_units(0, 1, JOINT_ROWS, joint_block)
    sent = steps(BEFORE_SEND)
    inner_units(1, sent, JOINT_ROWS, joint_block)
    pl.when(early)(start_early)
    ahead = steps(BEFORE_PLACES)
    inner_units(sent, ahead, JOINT_ROWS, joint_block)

    force_sum[...] = jnp.zeros_like(force_sum)
    force_other[...] = jnp.zeros_like(force_other)
    pos_copy.wait()
    vel_copy.start()

    @pl.when(early)
    def _():
        pl.semaphore_wait(left_sem, 3)
        edge_copies[2].start()
        edge_copies[5].start()

    shift_positions(2, [got_p[0] - 2.0] + [got_p[f] for f in range(1, 4)], False)
    outer_units(0, 3, OUTER_ROWS, lambda *args: pair_block(*args, 0, SLOTS, False, OUTER_UNROLL))
    back_d[...] = others_of(rho_other, 2)
    back_d_copy = send(8, back_d, got_d, -1, 0)

    inner_units(ahead, INNER, JOINT_ROWS, joint_block)

    for copy in edge_copies:
        copy.wait()
    left_half = lane_ids(1) < SLOTS

    def edge_rows(edge):
        inside = jnp.where(gy == 0, 0.0, 1.0) if edge == 0 else jnp.where(gy == gy_count - 1, 0.0, 1.0)
        shift = -1.0 if edge == 0 else 1.0
        blocks = []
        for block in range(2):
            rows = []
            for f in range(7):
                if block == 0:
                    row = edge_got[edge, 0, f : f + 1, :]
                else:
                    right = edge_got[edge, 2, f : f + 1, :]
                    left = edge_got[edge, 1, f : f + 1, :]
                    if f == 0:
                        right = right + 2.0
                        left = left - 2.0
                    row = jnp.where(left_half, right, left)
                if f == 1:
                    row = row + shift
                if f == 3:
                    row = row * inside
                rows.append(row)
            blocks.append(rows)
        return blocks

    def edge_lane(edge):
        return 0 if edge == 0 else LANES - 1

    def at_edge(total, col, lane):
        summed = jnp.sum(total, axis=1, keepdims=True) * near_p[col, 1, 3]
        return jnp.where(lane_ids(SLOTS) == lane, summed, 0.0)

    for edge in range(2):
        lane = edge_lane(edge)
        blocks = edge_rows(edge)
        for col in range(2):
            own = [near_p[col, 1, f][:, lane : lane + 1] for f in range(3)]
            total = jnp.zeros((SLOTS, LANES), F32)
            for near in blocks:
                _, dist, spline = spline_of([own[f] - near[f] for f in range(3)])
                spline_sq = spline * spline
                total = total + spline_sq * spline_sq * (dist + 0.25) * near[3]
            rho_sum[col] += at_edge(total, col, lane)

    def shift_densities(column, rho, first):
        for shift in (-1, 0, 1):
            if not (first and shift == 0):
                near_r[column, 1 + shift, 0] = shifted(rho, shift)
            near_r[column, 1 + shift, 1] = pressure_term(shifted(rho, shift))

    def occupied_of(col):
        mass = near_p[col, 1, 3]
        occupied = mass > 0.0
        return occupied, 1.0 / jnp.where(occupied, mass, 1.0)

    def finish_density(col, more):
        occupied, per_mass = occupied_of(col)
        rho = rho_sum[col] + others_of(rho_other, col)
        if more is not None:
            rho = rho + more
        rho = (4.0 * KERNEL_NORM) * rho * per_mass
        rho_out[pl.ds(col, SLOTS, stride=2), :] = jnp.where(occupied, rho, 0.0)
        near_r[col, 1, 0] = jnp.where(occupied, rho, 1.0)


    def force_block(unit, own_col, near_col, near_shift, other, first, count, near_first, near_count):
        rows = pl.ds(pl.multiple_of(first, 8), count)
        own = [near_p[own_col, 1, f, rows, :] for f in range(3)] + [near_r[own_col, 1, f, rows, :] for f in range(2)]

        def step(index, totals):
            j = near_first + index
            row = pl.ds(j, 1)
            near = [near_p[near_col, near_shift, f, row, :] for f in range(3)]
            near += [near_r[near_col, near_shift, f, row, :] for f in range(2)]
            weight = kept_a[unit, j, rows, :] * (own[4] + near[4])
            weight = weight + kept_b[unit, j, rows, :] / (own[3] + near[3])
            terms = [weight * (own[f] - near[f]) for f in range(3)]
            if other is not None:
                for f in range(3):
                    force_other[f, other, other_rows(j), :] += groups_sum(terms[f])
            return tuple(totals[f] + terms[f] for f in range(3))

        zeros = tuple(jnp.zeros((count, LANES), F32) for _ in range(3))
        totals = lax.fori_loop(0, near_count, step, zeros, unroll=FORCE_UNROLL)
        for f in range(3):
            force_sum[own_col, f, rows, :] += totals[f]

    def late_units(first, last):
        outer_units(
            first, last, JOINT_ROWS,
            lambda unit, own, near, shift, other, start, count: late_block(unit, own, near, shift, start, count),
        )

    finish_density(0, None)
    shift_densities(0, near_r[0, 1, 0], True)
    done = steps(BEFORE_DENSITY)
    one = steps((1, 0))
    same_cells(0, one, force_block)
    inner_units(0, one, FORCE_ROWS, force_block)
    vel_copy.wait()
    shift_velocities(2, [got_v[f] for f in range(3)], False)
    late_units(0, done)

    back_d_copy.wait()
    finish_density(1, got_d[...])
    rho_copy = send(9, near_r.at[1, 1, 0], got_r, 1, 0)
    own_rho = [[near_r[col, 1, 0]] for col in range(2)]
    for edge, lane in ((0, 0), (1, LANES - 1)):
        edge_rho[edge] = edge_pack(own_rho, lane)
    edge_rho_copies = edge_sends(10, edge_rho, edge_rho_got)
    for copy in edge_rho_copies:
        copy.start()
    shift_densities(1, near_r[1, 1, 0], True)

    late_units(done, 3)
    two = steps((2, 0))
    ahead = steps(BEFORE_FORCE)
    same_cells(one, two, force_block)
    inner_units(one, ahead, FORCE_ROWS, force_block)

    rho_copy.wait()
    shift_densities(2, got_r[...], False)
    back_f_copies = []
    for half in range(2):
        first, count = HALF * half, HALF
        outer_units(0, 3, FORCE_ROWS, lambda *args: force_block(*args, first, count))
        for f in range(3):
            back_f[half, f] = others_of(force_other.at[f], 2, first, count)
        back_f_copies.append(send(16 + half, back_f.at[half], got_f.at[half], -1, 0))

    same_cells(two, 2, force_block)
    inner_units(ahead, INNER, FORCE_ROWS, force_block)

    for copy in edge_rho_copies:
        copy.wait()
    for edge in range(2):
        lane = edge_lane(edge)
        blocks = edge_rows(edge)
        for block in range(2):
            if block == 0:
                rho = edge_rho_got[edge, 0, 0:1, :]
            else:
                rho = jnp.where(left_half, edge_rho_got[edge, 2, 0:1, :], edge_rho_got[edge, 1, 0:1, :])
            blocks[block] = blocks[block] + [rho, pressure_term(rho)]
        for col in range(2):
            own = [ref[col, 1, f][:, lane : lane + 1] for ref, n in ((near_p, 4), (near_v, 3), (near_r, 2)) for f in range(n)]
            totals = [jnp.zeros((SLOTS, LANES), F32) for _ in range(3)]
            for near in blocks:
                sep = [own[f] - near[f] for f in range(3)]
                dist_sq, _, spline = spline_of(sep)
                strength = own[8] + near[8] + approach_of(own, near, sep, dist_sq) / (own[7] + near[7])
                weight = strength * (spline * spline * spline) * near[3]
                totals = [totals[f] + weight * sep[f] for f in range(3)]
            for f in range(3):
                force_sum[col, f] += at_edge(totals[f], col, lane)

    for col in (0, 1):
        rows = pl.ds(col, SLOTS, stride=2)
        occupied, per_mass = occupied_of(col)
        row_id = (gy * LANES + lane_ids(SLOTS)).astype(F32)
        height = row_id + near_p[col, 1, 1]
        near_floor = jnp.maximum(1.0 - 2.0 * height, 0.0)
        near_ceiling = jnp.maximum(1.0 - 2.0 * (float(LANES * gy_count) - height), 0.0)
        push = WALL_STIFFNESS * (near_floor * near_floor - near_ceiling * near_ceiling)
        sums = [force_sum[col, f] - others_of(force_other.at[f], col) for f in range(3)]
        if col == 1:
            for copy in back_f_copies:
                copy.wait()
            sums = [sums[f] - jnp.concatenate([got_f[0, f], got_f[1, f]], axis=0) for f in range(3)]
        for f in range(3):
            force = (20.0 * KERNEL_NORM) * sums[f] * per_mass
            if f == 1:
                force = force + push
            acc_out[f, rows, :] = jnp.where(occupied, force, 0.0)


def on_device(gx_count, gy_count, position, velocity, particle_mass, counts):
    vmem = pl.BlockSpec(memory_space=pltpu.VMEM)
    anywhere = pl.BlockSpec(memory_space=pl.ANY)
    column = (SLOTS, LANES)
    others = len(OTHERS)
    rho, acceleration = pl.pallas_call(
        functools.partial(kernel, gx_count, gy_count),
        out_shape=(
            jax.ShapeDtypeStruct((2 * SLOTS, LANES), F32),
            jax.ShapeDtypeStruct((3, 2 * SLOTS, LANES), F32),
        ),
        in_specs=[anywhere] * 4,
        out_specs=(vmem, vmem),
        scratch_shapes=[
            pltpu.VMEM((3, 2 * SLOTS, LANES), F32),
            pltpu.VMEM((3, 2 * SLOTS, LANES), F32),
            pltpu.VMEM((2 * SLOTS, LANES), F32),
            pltpu.VMEM((2, LANES), jnp.int32),
            pltpu.VMEM((3, 3, 4) + column, F32),
            pltpu.VMEM((3, 3, 3) + column, F32),
            pltpu.VMEM((3, 3, 2) + column, F32),
            pltpu.VMEM((4,) + column, F32),
            pltpu.VMEM((3,) + column, F32),
            pltpu.VMEM(column, F32),
            pltpu.VMEM(column, F32),
            pltpu.VMEM(column, F32),
            pltpu.VMEM((2, 3, HALF, LANES), F32),
            pltpu.VMEM((2, 3, HALF, LANES), F32),
            pltpu.VMEM((2, 8, LANES), F32),
            pltpu.VMEM((2, 3, 8, LANES), F32),
            pltpu.VMEM((2, 8, LANES), F32),
            pltpu.VMEM((2, 3, 8, LANES), F32),
            pltpu.VMEM((UNITS, SLOTS) + column, F32),
            pltpu.VMEM((UNITS, SLOTS) + column, F32),
            pltpu.VMEM((2,) + column, F32),
            pltpu.VMEM((others, 8 * SLOTS, LANES), F32),
            pltpu.VMEM((2, 3) + column, F32),
            pltpu.VMEM((3, others, 8 * SLOTS, LANES), F32),
            pltpu.SemaphoreType.DMA((18,)),
            pltpu.SemaphoreType.DMA((18,)),
            pltpu.SemaphoreType.DMA((4,)),
            pltpu.SemaphoreType.REGULAR,
        ],
        compiler_params=pltpu.CompilerParams(
            collective_id=0, has_side_effects=True, vmem_limit_bytes=58 * 1024 * 1024
        ),
        cost_estimate=pl.CostEstimate(flops=400_000_000, bytes_accessed=2_000_000, transcendentals=30_000_000),
    )(
        position.reshape(3, 2 * SLOTS, LANES),
        velocity.reshape(3, 2 * SLOTS, LANES),
        particle_mass.reshape(2 * SLOTS, LANES),
        counts,
    )
    return rho.reshape(SLOTS, 2, LANES), acceleration.reshape(3, SLOTS, 2, LANES)


def solution(mesh):
    in_specs = (
        P(None, None, "gx", "gy"),
        P(None, None, "gx", "gy"),
        P(None, "gx", "gy"),
        P("gx", "gy"),
    )
    out_specs = (P(None, "gx", "gy"), P(None, None, "gx", "gy"))
    step = functools.partial(on_device, mesh.shape["gx"], mesh.shape["gy"])
    return jax.shard_map(step, mesh=mesh, in_specs=in_specs, out_specs=out_specs, check_vma=False)
```
